32 devices in a mesh: clus: 8 (over z, x), src: 4 (over y, core).
Axes of the slice: x: 2, y: 2, z: 4, core: 2. Of those that a mesh axis runs over, the one named last changes fastest.
Arguments:
- embeddings: float32 [4096, 768], P(('clus', 'src'))
- cluster: int32 [4096], P(('clus', 'src')), may hold values from 0 to 63, as said below
Outputs:
- centroids: float32 [64, 768], P('clus')
- nearest: float32 [4096], P(('clus', 'src'))
The draws below stay inside these ranges and needn't reach their ends.
Inputs may be any that keep to these rules, and one draw needn't show every extreme that they name: Of one device's 128 rows, at most 32 have clusters of one owner (cluster // 8); one owner receives exactly 32 rows from every device.
All inputs are finite; a program needn't handle non-finite values.
Results may differ from the reference program's by a relative error of at most 0.00032.
Values may be sent and summed in bfloat16 or wider, within the bound.
A program may use at most 64 MiB of HBM per device.

```python
import math
import jax
import jax.numpy as jnp
from jax import lax

D = 768
CLUS_DEV = 8
R_DEV = 128
CAP = 32
K = 64
ROWS = 4096
N_CLUS = 8
N_SRC = 4
DEVICES = 32


def owners_drawn(key):
    hottest = jax.random.randint(jax.random.fold_in(key, 11), (), 0, N_CLUS)
    block_keys = jax.random.split(jax.random.fold_in(key, 12), DEVICES)

    def one_block(block_key):
        first_key, second_key = jax.random.split(block_key)
        picked = jax.random.permutation(first_key, (N_CLUS - 1) * CAP)[:R_DEV - CAP]
        others = picked // CAP
        others = others + (others >= hottest).astype(others.dtype)
        owners = jnp.concatenate([jnp.full((CAP,), hottest, jnp.int32), others.astype(jnp.int32)])
        return owners[jax.random.permutation(second_key, R_DEV)]
    return jax.vmap(one_block)(block_keys).reshape(-1)


def clusters_drawn(key):
    owners = owners_drawn(key)
    within = jax.random.randint(jax.random.fold_in(key, 13), (ROWS,), 0, CLUS_DEV)
    return (owners * CLUS_DEV + within).astype(jnp.int32)


def draw_cluster(key, part):
    return clusters_drawn(key)


def draw_embeddings(key, part):
    labels = clusters_drawn(key)
    key = jax.random.fold_in(key, 3)
    base_key, scale_key, sign_key, noise_key = jax.random.split(key, 4)
    centers = jax.random.normal(base_key, (K, D), jnp.float32)
    strength = jnp.exp(jax.random.uniform(scale_key, (ROWS, 1), jnp.float32, math.log(0.2), math.log(3.0)))
    signs = (2 * jax.random.randint(sign_key, (ROWS, 1), 0, 2) - 1).astype(jnp.float32)
    noise = jax.random.normal(noise_key, (ROWS, D), jnp.float32)
    return (signs * strength * centers[labels] + noise).astype(jnp.float32)


def setup_inputs(seed: int = 0) -> dict:
    streams_of = jax.random.split(jax.random.key(seed), 3)
    embeddings = draw_embeddings(jax.random.fold_in(streams_of[2], 71), 0)
    cluster = draw_cluster(jax.random.fold_in(streams_of[2], 71), 0)
    return {"embeddings": embeddings, "cluster": cluster}


def reference(embeddings, cluster):
    sums = jax.ops.segment_sum(embeddings, cluster, num_segments=K)
    centroids = sums * lax.rsqrt(lax.optimization_barrier(jnp.sum(sums * sums, axis=1, keepdims=True)) + 1e-06)
    unit = (embeddings * lax.rsqrt(lax.optimization_barrier(jnp.sum(embeddings * embeddings, axis=1, keepdims=True)) + 1e-06)).astype(jnp.bfloat16)
    owner = (cluster // CLUS_DEV).astype(jnp.int32)
    order = jnp.argsort(owner, stable=True).astype(jnp.int32)
    counts = jax.ops.segment_sum(jnp.ones_like(owner), owner, num_segments=N_CLUS)
    starts = (jnp.cumsum(counts) - counts).astype(jnp.int32)
    window = N_SRC * N_CLUS * CAP
    padded_unit = jnp.concatenate([unit[order], jnp.zeros((window, D), jnp.bfloat16)], axis=0)
    padded_ids = jnp.concatenate([cluster[order], jnp.full((window,), -1, jnp.int32)], axis=0)

    def per_owner(index):
        first = starts[index]
        member_rows = lax.dynamic_slice(padded_unit, (first, jnp.zeros((), jnp.int32)), (window, D)).astype(jnp.float32)
        member_ids = lax.dynamic_slice(padded_ids, (first,), (window,))
        places = jnp.arange(window, dtype=jnp.int32)
        member_ids = jnp.where(places < counts[index], member_ids, -1)
        scores = jnp.dot(member_rows, member_rows.T, precision=lax.Precision.HIGHEST, preferred_element_type=jnp.float32)
        allowed = (member_ids[:, None] == member_ids[None, :]) & (places[:, None] != places[None, :]) & (member_ids[:, None] >= 0)
        return lax.optimization_barrier(jnp.max(jnp.where(allowed, scores, jnp.float32(-1.0)), axis=1))
    maxima = lax.map(per_owner, jnp.arange(N_CLUS, dtype=jnp.int32))
    sorted_owner = owner[order]
    local_place = jnp.arange(ROWS, dtype=jnp.int32) - starts[sorted_owner]
    values = maxima[sorted_owner, local_place]
    nearest = jnp.zeros((ROWS,), jnp.float32).at[order].set(values)
    return (centroids, nearest)
```

```python
import functools

import jax
import jax.numpy as jnp
from jax import lax
from jax.experimental import pallas as pl
from jax.experimental.pallas import tpu as pltpu
from jax.sharding import PartitionSpec as P

CLUS_DEV = 8
MESH = pl.DeviceIdType.MESH
EPS = 1e-06


def partner(index, distance, count):
    total = 0
    bit = 1
    while bit < count:
        value = (index // bit) % 2
        total = total + bit * ((1 - value) if (distance // bit) % 2 else value)
        bit *= 2
    return total


def exact_parts(values):
    high = values.astype(jnp.bfloat16)
    rest = values - high.astype(jnp.float32)
    middle = rest.astype(jnp.bfloat16)
    low = (rest - middle.astype(jnp.float32)).astype(jnp.bfloat16)
    return high, middle, low


def dot_t(left, right):
    return lax.dot_general(left, right, (((1,), (1,)), ((), ())), preferred_element_type=jnp.float32)


def own_lanes(rows_ref, n_clus, cap):
    width = n_clus * cap
    group = lax.broadcasted_iota(jnp.int32, (1, width), 1) // cap
    total = jnp.zeros((1, width), jnp.float32)
    for d in range(n_clus):
        total = jnp.where(group == d, rows_ref[d], total)
    return total


def owner_kernel(
    n_clus,
    n_src,
    cap,
    cluster_ref,
    emb_ref,
    cent_ref,
    near_ref,
    packed,
    gathered,
    labels,
    shard_labels,
    partial,
    partial_in,
    owned,
    owned_in,
    cents,
    maxima,
    row_sem,
    y_sem,
    core_sem,
    diag_sem,
    label_sem,
    shard_sem,
    partial_sem,
    owned_sem,
    cent_sem,
    max_sem,
):
    rows, depth = emb_ref.shape
    slots = n_clus * cap
    per = CLUS_DEV // n_src
    me = lax.axis_index("clus")
    src = lax.axis_index("src")
    clus_peer = [partner(me, d, n_clus) for d in range(n_clus)]
    src_peer = [partner(src, e, n_src) for e in range(n_src)]
    at_clus = [(clus_peer[d], src) for d in range(n_clus)]
    at_src = [(me, src_peer[e]) for e in range(n_src)]

    def copy(source, target, sems, slot, device):
        return pltpu.make_async_remote_copy(
            src_ref=source,
            dst_ref=target,
            send_sem=sems.at[0, slot],
            recv_sem=sems.at[1, slot],
            device_id=device,
            device_id_type=MESH,
        )

    barrier = pltpu.get_barrier_semaphore()
    others = [at_clus[d] for d in range(1, n_clus)] + [at_src[e] for e in range(1, n_src)]
    for device in others:
        pl.semaphore_signal(barrier, inc=1, device_id=device, device_id_type=MESH)

    cluster = cluster_ref[...]
    within = cluster % CLUS_DEV
    distance = jnp.bitwise_xor(cluster // CLUS_DEV, me)
    hits = lax.broadcasted_iota(jnp.int32, (n_clus, rows), 0) == distance
    earlier = lax.broadcasted_iota(jnp.int32, (rows, rows), 0) < lax.broadcasted_iota(
        jnp.int32, (rows, rows), 1
    )
    before = jnp.dot(
        jnp.where(hits, 1.0, 0.0).astype(jnp.bfloat16),
        jnp.where(earlier, 1.0, 0.0).astype(jnp.bfloat16),
        preferred_element_type=jnp.float32,
    )
    place = jnp.sum(jnp.where(hits, before, 0.0), axis=0, keepdims=True).astype(jnp.int32)
    slot = distance * cap + place
    pick = jnp.where(lax.broadcasted_iota(jnp.int32, (slots, rows), 0) == slot, 1.0, 0.0).astype(
        jnp.bfloat16
    )

    emb = emb_ref[...]
    unit = (emb * lax.rsqrt(jnp.sum(emb * emb, axis=1, keepdims=True) + EPS)).astype(jnp.bfloat16)
    packed[...] = (
        jnp.dot(pick, unit, preferred_element_type=jnp.float32)
        .astype(jnp.bfloat16)
        .reshape(n_clus, cap, depth)
    )
    gathered[0, 0] = packed[0]
    label_row = dot_t(
        jnp.broadcast_to((within + 1).astype(jnp.float32), (8, rows)).astype(jnp.bfloat16), pick
    )[:1]
    labels[0] = label_row

    label_copy = {
        d: copy(labels.at[0], labels.at[d], label_sem, d, at_clus[d]) for d in range(1, n_clus)
    }
    row_copy = {
        d: copy(packed.at[d], gathered.at[0, d], row_sem, d, at_clus[d]) for d in range(1, n_clus)
    }
    core_copy = {
        d: copy(gathered.at[0, d], gathered.at[1, d], core_sem, d, at_src[1]) for d in range(n_clus)
    }
    y_copy = {
        d: copy(gathered.at[0, d], gathered.at[2, d], y_sem, d, at_src[2]) for d in range(n_clus)
    }
    diag_copy = {
        d: copy(gathered.at[2, d], gathered.at[3, d], diag_sem, d, at_src[1]) for d in range(n_clus)
    }
    partial_copy = {
        e: copy(partial.at[e], partial_in.at[e], partial_sem, e, at_src[e]) for e in range(1, n_src)
    }
    owned_copy = {
        d: copy(owned.at[d], owned_in.at[d], owned_sem, d, at_clus[d]) for d in range(1, n_clus)
    }
    cent_copy = {
        e: copy(cents.at[0], cents.at[e], cent_sem, e, at_src[e]) for e in range(1, n_src)
    }
    shard_copy = {
        e: copy(shard_labels.at[0], shard_labels.at[e], shard_sem, e, at_src[e])
        for e in range(1, n_src)
    }
    max_copy = {
        d: copy(maxima.at[0], maxima.at[d], max_sem, d, at_clus[d]) for d in range(1, n_clus)
    }

    pl.semaphore_wait(barrier, len(others))
    far_first = sorted(range(1, n_clus), key=lambda d: -d)
    near_first = sorted(range(1, n_clus))
    y_copy[0].start()
    for d in far_first:
        row_copy[d].start()
    core_copy[0].start()
    for d in near_first:
        label_copy[d].start()

    order = (
        jnp.bitwise_xor(within // per, src) * (n_clus * per) + distance * per + within % per
    )
    count = n_src * n_clus * per
    members = jnp.where(
        lax.broadcasted_iota(jnp.int32, (count, rows), 0) == order, 2.0, 0.0
    ).astype(jnp.bfloat16)
    sums = jnp.zeros((count, depth), jnp.float32)
    for part in exact_parts(emb * 0.5):
        sums = sums + jnp.dot(members, part, preferred_element_type=jnp.float32)
    partial[...] = sums.reshape(n_src, n_clus * per, depth)
    for e in range(1, n_src):
        partial_copy[e].start()

    for d in near_first:
        label_copy[d].wait_recv()
    own_labels = own_lanes(labels, n_clus, cap)
    shard_labels[0] = own_labels
    for e in range(1, n_src):
        shard_copy[e].start()

    def reduce_sums():
        total = partial[0]
        for e in range(1, n_src):
            partial_copy[e].wait_recv()
            total = total + partial_in[e]
        for d in range(n_clus):
            owned[d] = total[d * per : (d + 1) * per]
        for d in range(1, n_clus):
            owned_copy[d].start()

    def finish_sums():
        total = owned[0]
        for d in range(1, n_clus):
            owned_copy[d].wait_recv()
            total = total + owned_in[d]
        cents[0] = total * lax.rsqrt(jnp.sum(total * total, axis=1, keepdims=True) + EPS)
        for e in range(1, n_src):
            cent_copy[e].start()

    def shard_maxima(e):
        scores = dot_t(gathered[e].reshape(slots, depth), gathered[0].reshape(slots, depth))
        other = jnp.transpose(jnp.broadcast_to(shard_labels[e], (128, slots)))
        other = jnp.concatenate([other] * (slots // 128), axis=1)
        allowed = other == own_labels
        if e == 0:
            allowed = allowed & (
                lax.broadcasted_iota(jnp.int32, (slots, slots), 0)
                != lax.broadcasted_iota(jnp.int32, (slots, slots), 1)
            )
        return jnp.max(jnp.where(allowed, scores, -1.0), axis=0, keepdims=True)

    waiting = [0]
    for step, d in enumerate(near_first):
        row_copy[d].wait_recv()
        y_copy[d].start()
        core_copy[d].start()
        waiting.append(d)
        if step == 1:
            reduce_sums()
        if step >= 2:
            first = waiting.pop(0)
            y_copy[first].wait_recv()
            diag_copy[first].start()
    best = shard_maxima(0)
    finish_sums()
    for d in waiting:
        y_copy[d].wait_recv()
        diag_copy[d].start()
    for e in range(1, n_src):
        shard_copy[e].wait_recv()
    best = jnp.maximum(best, shard_maxima(2))
    for d in range(n_clus):
        core_copy[d].wait_recv()
    best = jnp.maximum(best, shard_maxima(1))
    for d in range(n_clus):
        diag_copy[d].wait_recv()
    maxima[0] = jnp.maximum(best, shard_maxima(3))
    for d in far_first:
        max_copy[d].start()

    for e in range(1, n_src):
        cent_copy[e].wait_recv()
    for shard in range(n_src):
        cent_ref[shard * per : (shard + 1) * per, :] = cents[src_peer[shard]]
    for d in near_first:
        max_copy[d].wait_recv()
    near = jnp.zeros((8, rows), jnp.float32)
    for part in exact_parts(jnp.broadcast_to(own_lanes(maxima, n_clus, cap), (8, slots))):
        near = near + jnp.dot(part, pick, preferred_element_type=jnp.float32)
    near_ref[...] = near[:1]

    for copies in (
        label_copy,
        row_copy,
        core_copy,
        y_copy,
        diag_copy,
        partial_copy,
        shard_copy,
        owned_copy,
        cent_copy,
        max_copy,
    ):
        for started in copies.values():
            started.wait_send()


def one_kernel(n_clus, n_src, embeddings, cluster):
    rows, depth = embeddings.shape
    cap = 2 * rows // n_clus
    slots = n_clus * cap
    per = CLUS_DEV // n_src
    f32, bf16 = jnp.float32, jnp.bfloat16
    vmem = pl.BlockSpec(memory_space=pltpu.VMEM)
    centroids, nearest = pl.pallas_call(
        functools.partial(owner_kernel, n_clus, n_src, cap),
        out_shape=(
            jax.ShapeDtypeStruct((CLUS_DEV, depth), f32),
            jax.ShapeDtypeStruct((1, rows), f32),
        ),
        in_specs=[vmem, vmem],
        out_specs=(vmem, vmem),
        scratch_shapes=[
            pltpu.VMEM((n_clus, cap, depth), bf16),
            pltpu.VMEM((n_src, n_clus, cap, depth), bf16),
            pltpu.VMEM((n_clus, 1, slots), f32),
            pltpu.VMEM((n_src, 1, slots), f32),
            pltpu.VMEM((n_src, n_clus * per, depth), f32),
            pltpu.VMEM((n_src, n_clus * per, depth), f32),
            pltpu.VMEM((n_clus, per, depth), f32),
            pltpu.VMEM((n_clus, per, depth), f32),
            pltpu.VMEM((n_src, per, depth), f32),
            pltpu.VMEM((n_clus, 1, slots), f32),
        ]
        + [
            pltpu.SemaphoreType.DMA((2, count))
            for count in (n_clus, n_clus, n_clus, n_clus, n_clus, n_src, n_src, n_clus, n_src, n_clus)
        ],
        compiler_params=pltpu.CompilerParams(
            collective_id=0, has_side_effects=True, vmem_limit_bytes=32 * 1024 * 1024
        ),
        cost_estimate=pl.CostEstimate(
            flops=2 * slots * slots * n_src * depth, bytes_accessed=rows * depth * 4, transcendentals=0
        ),
    )(cluster.reshape(1, rows), embeddings)
    return centroids, nearest.reshape(rows)


def block_maxima(current, own_unit, own_labels, own_global, other_unit, other_labels, other_global):
    scores = lax.dot_general(
        own_unit, other_unit, (((1,), (1,)), ((), ())), preferred_element_type=jnp.float32
    )
    allowed = (
        (own_labels[:, None] == other_labels[None, :])
        & (own_global[:, None] != other_global[None, :])
        & (own_labels[:, None] >= 0)
    )
    return jnp.maximum(current, jnp.max(jnp.where(allowed, scores, jnp.float32(-1.0)), axis=1))


def unit_rows(values):
    return (values * lax.rsqrt(jnp.sum(values * values, axis=1, keepdims=True) + 1e-06)).astype(
        jnp.bfloat16
    )


def normalized(owned):
    return owned * lax.rsqrt(jnp.sum(owned * owned, axis=1, keepdims=True) + 1e-06)


def on_device(embeddings, cluster):
    row_count = embeddings.shape[0]
    feature_dim = embeddings.shape[1]
    clus_count = lax.axis_size("clus")
    source_count = lax.axis_size("src")
    capacity = max(2, 2 * row_count // clus_count)
    slot_total = clus_count * capacity
    owner = cluster // CLUS_DEV
    member_hits = (owner[:, None] == jnp.arange(clus_count, dtype=jnp.int32)[None, :]).astype(
        jnp.int32
    )
    running = jnp.cumsum(member_hits, axis=0)
    position = jnp.sum(member_hits * running, axis=1) - 1
    slot_index = owner * capacity + position
    device_number = lax.axis_index("clus") * source_count + lax.axis_index("src")
    global_row = device_number * row_count + jnp.arange(row_count, dtype=jnp.int32)
    send_labels = jnp.full((slot_total,), -1, jnp.int32).at[slot_index].set(cluster)
    send_global = jnp.full((slot_total,), -1, jnp.int32).at[slot_index].set(global_row)
    count = lax.axis_size("clus") * CLUS_DEV
    inside = (cluster >= 0) & (cluster < count)
    segment = jnp.where(inside, cluster, count)
    owned = lax.psum_scatter(
        jax.ops.segment_sum(embeddings, segment, num_segments=count + 1)[:count],
        "clus",
        scatter_dimension=0,
        tiled=True,
    )
    owned = lax.psum(owned, "src")
    centroids = normalized(owned)
    unit = unit_rows(embeddings)
    send_unit = jnp.zeros((slot_total, feature_dim), jnp.bfloat16).at[slot_index].set(unit)
    received, recv_labels, recv_global = (
        lax.all_to_all(send_unit, "clus", split_axis=0, concat_axis=0, tiled=True),
        lax.all_to_all(send_labels, "clus", split_axis=0, concat_axis=0, tiled=True),
        lax.all_to_all(send_global, "clus", split_axis=0, concat_axis=0, tiled=True),
    )
    initial = jnp.full((slot_total,), -1.0, jnp.float32)
    piece_unit = lax.all_gather(received, "src", axis=0, tiled=True)
    piece_labels = lax.all_gather(recv_labels, "src", axis=0, tiled=True)
    piece_global = lax.all_gather(recv_global, "src", axis=0, tiled=True)
    length = piece_unit.shape[0]
    stacked = (
        piece_unit.reshape(length // slot_total, slot_total, feature_dim),
        piece_labels.reshape(length // slot_total, slot_total),
        piece_global.reshape(length // slot_total, slot_total),
    )

    def stepper(carried, sliced):
        return (
            block_maxima(
                carried, received, recv_labels, recv_global, sliced[0], sliced[1], sliced[2]
            ),
            None,
        )

    result, unused = lax.scan(stepper, initial, stacked)
    returned = lax.all_to_all(result, "clus", split_axis=0, concat_axis=0, tiled=True)
    nearest = returned[slot_index]
    return (centroids, nearest)


def fits_one_kernel(n_clus, n_src, rows):
    cap = 2 * rows // n_clus
    return (
        n_src == 4
        and n_clus & (n_clus - 1) == 0
        and cap % 16 == 0
        and n_clus * cap % 128 == 0
        and rows % 128 == 0
    )


def solution(mesh):
    n_clus, n_src = mesh.shape["clus"], mesh.shape["src"]

    def body(embeddings, cluster):
        if fits_one_kernel(n_clus, n_src, embeddings.shape[0]):
            return one_kernel(n_clus, n_src, embeddings, cluster)
        return on_device(embeddings, cluster)

    placed = (P(("clus", "src"), None), P(("clus", "src")))
    return jax.shard_map(
        body,
        mesh=mesh,
        in_specs=placed,
        out_specs=(P("clus", None), P(("clus", "src"))),
        check_vma=False,
    )
```

```python
import functools

import jax
import jax.numpy as jnp
from jax import lax
from jax.experimental import pallas as pl
from jax.experimental.pallas import tpu as pltpu
from jax.sharding import PartitionSpec as P

CLUS_DEV = 8
MESH = pl.DeviceIdType.MESH
EPS = 1e-06


def partner(index, distance, count):
    total = 0
    bit = 1
    while bit < count:
        value = (index // bit) % 2
        total = total + bit * ((1 - value) if (distance // bit) % 2 else value)
        bit *= 2
    return total


def exact_parts(values):
    high = values.astype(jnp.bfloat16)
    rest = values - high.astype(jnp.float32)
    middle = rest.astype(jnp.bfloat16)
    low = (rest - middle.astype(jnp.float32)).astype(jnp.bfloat16)
    return high, middle, low


def dot_t(left, right):
    return lax.dot_general(left, right, (((1,), (1,)), ((), ())), preferred_element_type=jnp.float32)


def own_lanes(rows_ref, n_clus, cap):
    width = n_clus * cap
    group = lax.broadcasted_iota(jnp.int32, (1, width), 1) // cap
    total = jnp.zeros((1, width), jnp.float32)
    for d in range(n_clus):
        total = jnp.where(group == d, rows_ref[d], total)
    return total


def owner_kernel(
    n_clus,
    n_src,
    cap,
    cluster_hbm,
    emb_hbm,
    cent_ref,
    near_ref,
    cluster_ref,
    emb_ref,
    packed,
    gathered,
    labels,
    shard_labels,
    partial,
    partial_in,
    owned,
    owned_in,
    cents,
    maxima,
    row_sem,
    y_sem,
    core_sem,
    diag_sem,
    label_sem,
    shard_sem,
    partial_sem,
    owned_sem,
    cent_sem,
    max_sem,
    load_sem,
):
    rows, depth = emb_ref.shape
    slots = n_clus * cap
    per = CLUS_DEV // n_src
    me = lax.axis_index("clus")
    src = lax.axis_index("src")
    clus_peer = [partner(me, d, n_clus) for d in range(n_clus)]
    src_peer = [partner(src, e, n_src) for e in range(n_src)]
    at_clus = [(clus_peer[d], src) for d in range(n_clus)]
    at_src = [(me, src_peer[e]) for e in range(n_src)]

    def copy(source, target, sems, slot, device):
        return pltpu.make_async_remote_copy(
            src_ref=source,
            dst_ref=target,
            send_sem=sems.at[0, slot],
            recv_sem=sems.at[1, slot],
            device_id=device,
            device_id_type=MESH,
        )

    load_cluster = pltpu.make_async_copy(cluster_hbm, cluster_ref, load_sem.at[0])
    load_rows = pltpu.make_async_copy(emb_hbm, emb_ref, load_sem.at[1])
    load_cluster.start()
    load_rows.start()
    barrier = pltpu.get_barrier_semaphore()
    others = [at_clus[d] for d in range(1, n_clus)] + [at_src[e] for e in range(1, n_src)]
    for device in others:
        pl.semaphore_signal(barrier, inc=1, device_id=device, device_id_type=MESH)

    load_cluster.wait()
    cluster = cluster_ref[...]
    within = cluster % CLUS_DEV
    distance = jnp.bitwise_xor(cluster // CLUS_DEV, me)
    hits = lax.broadcasted_iota(jnp.int32, (n_clus, rows), 0) == distance
    earlier = lax.broadcasted_iota(jnp.int32, (rows, rows), 0) < lax.broadcasted_iota(
        jnp.int32, (rows, rows), 1
    )
    before = jnp.dot(
        jnp.where(hits, 1.0, 0.0).astype(jnp.bfloat16),
        jnp.where(earlier, 1.0, 0.0).astype(jnp.bfloat16),
        preferred_element_type=jnp.float32,
    )
    place = jnp.sum(jnp.where(hits, before, 0.0), axis=0, keepdims=True).astype(jnp.int32)
    slot = distance * cap + place
    pick = jnp.where(lax.broadcasted_iota(jnp.int32, (slots, rows), 0) == slot, 1.0, 0.0).astype(
        jnp.bfloat16
    )

    load_rows.wait()
    emb = emb_ref[...]
    unit = (emb * lax.rsqrt(jnp.sum(emb * emb, axis=1, keepdims=True) + EPS)).astype(jnp.bfloat16)
    packed[...] = (
        jnp.dot(pick, unit, preferred_element_type=jnp.float32)
        .astype(jnp.bfloat16)
        .reshape(n_clus, cap, depth)
    )
    gathered[0, 0] = packed[0]
    label_row = dot_t(
        jnp.broadcast_to((within + 1).astype(jnp.float32), (8, rows)).astype(jnp.bfloat16), pick
    )[:1]
    labels[0] = label_row

    label_copy = {
        d: copy(labels.at[0], labels.at[d], label_sem, d, at_clus[d]) for d in range(1, n_clus)
    }
    row_copy = {
        d: copy(packed.at[d], gathered.at[0, d], row_sem, d, at_clus[d]) for d in range(1, n_clus)
    }
    core_copy = {
        d: copy(gathered.at[0, d], gathered.at[1, d], core_sem, d, at_src[1]) for d in range(n_clus)
    }
    y_copy = {
        d: copy(gathered.at[0, d], gathered.at[2, d], y_sem, d, at_src[2]) for d in range(n_clus)
    }
    diag_copy = {
        d: copy(gathered.at[2, d], gathered.at[3, d], diag_sem, d, at_src[1]) for d in range(n_clus)
    }
    partial_copy = {
        e: copy(partial.at[e], partial_in.at[e], partial_sem, e, at_src[e]) for e in range(1, n_src)
    }
    owned_copy = {
        d: copy(owned.at[d], owned_in.at[d], owned_sem, d, at_clus[d]) for d in range(1, n_clus)
    }
    cent_copy = {
        e: copy(cents.at[0], cents.at[e], cent_sem, e, at_src[e]) for e in range(1, n_src)
    }
    shard_copy = {
        e: copy(shard_labels.at[0], shard_labels.at[e], shard_sem, e, at_src[e])
        for e in range(1, n_src)
    }
    max_copy = {
        d: copy(maxima.at[0], maxima.at[d], max_sem, d, at_clus[d]) for d in range(1, n_clus)
    }

    pl.semaphore_wait(barrier, len(others))
    half = n_clus // 2
    turns = [d for near in range(half) for d in (half + near, near + 1)][: n_clus - 1]
    for d in turns:
        label_copy[d].start()
    y_copy[0].start()
    for d in turns:
        row_copy[d].start()
    core_copy[0].start()

    order = (
        jnp.bitwise_xor(within // per, src) * (n_clus * per) + distance * per + within % per
    )
    count = n_src * n_clus * per
    members = jnp.where(
        lax.broadcasted_iota(jnp.int32, (count, rows), 0) == order, 2.0, 0.0
    ).astype(jnp.bfloat16)
    sums = jnp.zeros((count, depth), jnp.float32)
    for part in exact_parts(emb * 0.5):
        sums = sums + jnp.dot(members, part, preferred_element_type=jnp.float32)
    partial[...] = sums.reshape(n_src, n_clus * per, depth)
    for e in range(1, n_src):
        partial_copy[e].start()

    def send_labels():
        for d in turns:
            label_copy[d].wait_recv()
        own_labels = own_lanes(labels, n_clus, cap)
        shard_labels[0] = own_labels
        for e in range(1, n_src):
            shard_copy[e].start()
        return own_labels

    def reduce_sums():
        total = partial[0]
        for e in range(1, n_src):
            partial_copy[e].wait_recv()
            total = total + partial_in[e]
        for d in range(n_clus):
            owned[d] = total[d * per : (d + 1) * per]
        for d in range(1, n_clus):
            owned_copy[d].start()

    def finish_sums():
        total = owned[0]
        for d in range(1, n_clus):
            owned_copy[d].wait_recv()
            total = total + owned_in[d]
        cents[0] = total * lax.rsqrt(jnp.sum(total * total, axis=1, keepdims=True) + EPS)
        for e in range(1, n_src):
            cent_copy[e].start()

    def shard_maxima(e):
        scores = dot_t(gathered[e].reshape(slots, depth), gathered[0].reshape(slots, depth))
        other = jnp.transpose(jnp.broadcast_to(shard_labels[e], (128, slots)))
        other = jnp.concatenate([other] * (slots // 128), axis=1)
        allowed = other == own_labels
        if e == 0:
            allowed = allowed & (
                lax.broadcasted_iota(jnp.int32, (slots, slots), 0)
                != lax.broadcasted_iota(jnp.int32, (slots, slots), 1)
            )
        return jnp.max(jnp.where(allowed, scores, -1.0), axis=0, keepdims=True)

    def pass_on(d):
        y_copy[d].wait_recv()
        diag_copy[d].start()

    waiting = [0]
    for step, d in enumerate(turns):
        row_copy[d].wait_recv()
        y_copy[d].start()
        core_copy[d].start()
        waiting.append(d)
        if step == 1:
            own_labels = send_labels()
        if step == 2:
            reduce_sums()
        if step >= 2:
            pass_on(waiting.pop(0))
    pass_on(waiting.pop(0))
    best = shard_maxima(0)
    for e in range(1, n_src):
        shard_copy[e].wait_recv()
    for d in range(n_clus):
        core_copy[d].wait_recv()
    best = jnp.maximum(best, shard_maxima(1))
    for d in waiting:
        pass_on(d)
    finish_sums()
    best = jnp.maximum(best, shard_maxima(2))
    for d in range(n_clus):
        diag_copy[d].wait_recv()
    maxima[0] = jnp.maximum(best, shard_maxima(3))
    for d in turns:
        max_copy[d].start()

    for e in range(1, n_src):
        cent_copy[e].wait_recv()
    for shard in range(n_src):
        cent_ref[shard * per : (shard + 1) * per, :] = cents[src_peer[shard]]
    for d in turns:
        max_copy[d].wait_recv()
    near = jnp.zeros((8, rows), jnp.float32)
    for part in exact_parts(jnp.broadcast_to(own_lanes(maxima, n_clus, cap), (8, slots))):
        near = near + jnp.dot(part, pick, preferred_element_type=jnp.float32)
    near_ref[...] = near[:1]

    for copies in (
        label_copy,
        row_copy,
        core_copy,
        y_copy,
        diag_copy,
        partial_copy,
        shard_copy,
        owned_copy,
        cent_copy,
        max_copy,
    ):
        for started in copies.values():
            started.wait_send()


def one_kernel(n_clus, n_src, embeddings, cluster):
    rows, depth = embeddings.shape
    cap = 2 * rows // n_clus
    slots = n_clus * cap
    per = CLUS_DEV // n_src
    f32, bf16 = jnp.float32, jnp.bfloat16
    vmem = pl.BlockSpec(memory_space=pltpu.VMEM)
    hbm = pl.BlockSpec(memory_space=pltpu.HBM)
    centroids, nearest = pl.pallas_call(
        functools.partial(owner_kernel, n_clus, n_src, cap),
        out_shape=(
            jax.ShapeDtypeStruct((CLUS_DEV, depth), f32),
            jax.ShapeDtypeStruct((1, rows), f32),
        ),
        in_specs=[hbm, hbm],
        out_specs=(vmem, vmem),
        scratch_shapes=[
            pltpu.VMEM((1, rows), jnp.int32),
            pltpu.VMEM((rows, depth), f32),
            pltpu.VMEM((n_clus, cap, depth), bf16),
            pltpu.VMEM((n_src, n_clus, cap, depth), bf16),
            pltpu.VMEM((n_clus, 1, slots), f32),
            pltpu.VMEM((n_src, 1, slots), f32),
            pltpu.VMEM((n_src, n_clus * per, depth), f32),
            pltpu.VMEM((n_src, n_clus * per, depth), f32),
            pltpu.VMEM((n_clus, per, depth), f32),
            pltpu.VMEM((n_clus, per, depth), f32),
            pltpu.VMEM((n_src, per, depth), f32),
            pltpu.VMEM((n_clus, 1, slots), f32),
        ]
        + [
            pltpu.SemaphoreType.DMA((2, count))
            for count in (n_clus, n_clus, n_clus, n_clus, n_clus, n_src, n_src, n_clus, n_src, n_clus)
        ]
        + [pltpu.SemaphoreType.DMA((2,))],
        compiler_params=pltpu.CompilerParams(
            collective_id=0, has_side_effects=True, vmem_limit_bytes=56 * 1024 * 1024
        ),
        cost_estimate=pl.CostEstimate(
            flops=2 * slots * slots * n_src * depth, bytes_accessed=rows * depth * 4, transcendentals=0
        ),
    )(cluster.reshape(1, rows), embeddings)
    return centroids, nearest.reshape(rows)


def block_maxima(current, own_unit, own_labels, own_global, other_unit, other_labels, other_global):
    scores = lax.dot_general(
        own_unit, other_unit, (((1,), (1,)), ((), ())), preferred_element_type=jnp.float32
    )
    allowed = (
        (own_labels[:, None] == other_labels[None, :])
        & (own_global[:, None] != other_global[None, :])
        & (own_labels[:, None] >= 0)
    )
    return jnp.maximum(current, jnp.max(jnp.where(allowed, scores, jnp.float32(-1.0)), axis=1))


def unit_rows(values):
    return (values * lax.rsqrt(jnp.sum(values * values, axis=1, keepdims=True) + 1e-06)).astype(
        jnp.bfloat16
    )


def normalized(owned):
    return owned * lax.rsqrt(jnp.sum(owned * owned, axis=1, keepdims=True) + 1e-06)


def on_device(embeddings, cluster):
    row_count = embeddings.shape[0]
    feature_dim = embeddings.shape[1]
    clus_count = lax.axis_size("clus")
    source_count = lax.axis_size("src")
    capacity = max(2, 2 * row_count // clus_count)
    slot_total = clus_count * capacity
    owner = cluster // CLUS_DEV
    member_hits = (owner[:, None] == jnp.arange(clus_count, dtype=jnp.int32)[None, :]).astype(
        jnp.int32
    )
    running = jnp.cumsum(member_hits, axis=0)
    position = jnp.sum(member_hits * running, axis=1) - 1
    slot_index = owner * capacity + position
    device_number = lax.axis_index("clus") * source_count + lax.axis_index("src")
    global_row = device_number * row_count + jnp.arange(row_count, dtype=jnp.int32)
    send_labels = jnp.full((slot_total,), -1, jnp.int32).at[slot_index].set(cluster)
    send_global = jnp.full((slot_total,), -1, jnp.int32).at[slot_index].set(global_row)
    count = lax.axis_size("clus") * CLUS_DEV
    inside = (cluster >= 0) & (cluster < count)
    segment = jnp.where(inside, cluster, count)
    owned = lax.psum_scatter(
        jax.ops.segment_sum(embeddings, segment, num_segments=count + 1)[:count],
        "clus",
        scatter_dimension=0,
        tiled=True,
    )
    owned = lax.psum(owned, "src")
    centroids = normalized(owned)
    unit = unit_rows(embeddings)
    send_unit = jnp.zeros((slot_total, feature_dim), jnp.bfloat16).at[slot_index].set(unit)
    received, recv_labels, recv_global = (
        lax.all_to_all(send_unit, "clus", split_axis=0, concat_axis=0, tiled=True),
        lax.all_to_all(send_labels, "clus", split_axis=0, concat_axis=0, tiled=True),
        lax.all_to_all(send_global, "clus", split_axis=0, concat_axis=0, tiled=True),
    )
    initial = jnp.full((slot_total,), -1.0, jnp.float32)
    piece_unit = lax.all_gather(received, "src", axis=0, tiled=True)
    piece_labels = lax.all_gather(recv_labels, "src", axis=0, tiled=True)
    piece_global = lax.all_gather(recv_global, "src", axis=0, tiled=True)
    length = piece_unit.shape[0]
    stacked = (
        piece_unit.reshape(length // slot_total, slot_total, feature_dim),
        piece_labels.reshape(length // slot_total, slot_total),
        piece_global.reshape(length // slot_total, slot_total),
    )

    def stepper(carried, sliced):
        return (
            block_maxima(
                carried, received, recv_labels, recv_global, sliced[0], sliced[1], sliced[2]
            ),
            None,
        )

    result, unused = lax.scan(stepper, initial, stacked)
    returned = lax.all_to_all(result, "clus", split_axis=0, concat_axis=0, tiled=True)
    nearest = returned[slot_index]
    return (centroids, nearest)


def fits_one_kernel(n_clus, n_src, rows):
    cap = 2 * rows // n_clus
    return (
        n_src == 4
        and n_clus & (n_clus - 1) == 0
        and cap % 16 == 0
        and n_clus * cap % 128 == 0
        and rows % 128 == 0
    )


def solution(mesh):
    n_clus, n_src = mesh.shape["clus"], mesh.shape["src"]

    def body(embeddings, cluster):
        if fits_one_kernel(n_clus, n_src, embeddings.shape[0]):
            return one_kernel(n_clus, n_src, embeddings, cluster)
        return on_device(embeddings, cluster)

    placed = (P(("clus", "src"), None), P(("clus", "src")))
    return jax.shard_map(
        body,
        mesh=mesh,
        in_specs=placed,
        out_specs=(P("clus", None), P(("clus", "src"))),
        check_vma=False,
    )
```

```python
import functools

import jax
import jax.numpy as jnp
from jax import lax
from jax.experimental import pallas as pl
from jax.experimental.pallas import tpu as pltpu
from jax.sharding import PartitionSpec as P

CLUS_DEV = 8
MESH = pl.DeviceIdType.MESH
EPS = 1e-06


def partner(index, distance, count):
    total = 0
    bit = 1
    while bit < count:
        value = (index // bit) % 2
        total = total + bit * ((1 - value) if (distance // bit) % 2 else value)
        bit *= 2
    return total


def exact_parts(values):
    high = values.astype(jnp.bfloat16)
    rest = values - high.astype(jnp.float32)
    middle = rest.astype(jnp.bfloat16)
    low = (rest - middle.astype(jnp.float32)).astype(jnp.bfloat16)
    return high, middle, low


def dot_t(left, right):
    return lax.dot_general(left, right, (((1,), (1,)), ((), ())), preferred_element_type=jnp.float32)


def own_lanes(rows_ref, n_clus, cap):
    width = n_clus * cap
    group = lax.broadcasted_iota(jnp.int32, (1, width), 1) // cap
    total = jnp.zeros((1, width), jnp.float32)
    for d in range(n_clus):
        total = jnp.where(group == d, rows_ref[d], total)
    return total


def owner_kernel(
    n_clus,
    n_src,
    cap,
    cluster_hbm,
    emb_hbm,
    cent_ref,
    near_ref,
    cluster_ref,
    emb_ref,
    packed,
    gathered,
    labels,
    shard_labels,
    partial,
    partial_in,
    owned,
    owned_in,
    cents,
    maxima,
    row_sem,
    y_sem,
    core_sem,
    diag_sem,
    label_sem,
    shard_sem,
    partial_sem,
    owned_sem,
    cent_sem,
    max_sem,
    load_sem,
):
    rows, depth = emb_ref.shape
    slots = n_clus * cap
    per = CLUS_DEV // n_src
    me = lax.axis_index("clus")
    src = lax.axis_index("src")
    clus_peer = [partner(me, d, n_clus) for d in range(n_clus)]
    src_peer = [partner(src, e, n_src) for e in range(n_src)]
    at_clus = [(clus_peer[d], src) for d in range(n_clus)]
    at_src = [(me, src_peer[e]) for e in range(n_src)]

    def copy(source, target, sems, slot, device):
        return pltpu.make_async_remote_copy(
            src_ref=source,
            dst_ref=target,
            send_sem=sems.at[0, slot],
            recv_sem=sems.at[1, slot],
            device_id=device,
            device_id_type=MESH,
        )

    load_cluster = pltpu.make_async_copy(cluster_hbm, cluster_ref, load_sem.at[0])
    load_rows = pltpu.make_async_copy(emb_hbm, emb_ref, load_sem.at[1])
    load_cluster.start()
    load_rows.start()
    barrier = pltpu.get_barrier_semaphore()
    others = [at_clus[d] for d in range(1, n_clus)] + [at_src[e] for e in range(1, n_src)]
    for device in others:
        pl.semaphore_signal(barrier, inc=1, device_id=device, device_id_type=MESH)

    load_cluster.wait()
    cluster = cluster_ref[...]
    within = cluster % CLUS_DEV
    distance = jnp.bitwise_xor(cluster // CLUS_DEV, me)
    hits = lax.broadcasted_iota(jnp.int32, (n_clus, rows), 0) == distance
    earlier = lax.broadcasted_iota(jnp.int32, (rows, rows), 0) < lax.broadcasted_iota(
        jnp.int32, (rows, rows), 1
    )
    before = jnp.dot(
        jnp.where(hits, 1.0, 0.0).astype(jnp.bfloat16),
        jnp.where(earlier, 1.0, 0.0).astype(jnp.bfloat16),
        preferred_element_type=jnp.float32,
    )
    place = jnp.sum(jnp.where(hits, before, 0.0), axis=0, keepdims=True).astype(jnp.int32)
    slot = distance * cap + place
    pick = jnp.where(lax.broadcasted_iota(jnp.int32, (slots, rows), 0) == slot, 1.0, 0.0).astype(
        jnp.bfloat16
    )

    load_rows.wait()
    emb = emb_ref[...]
    unit = (emb * lax.rsqrt(jnp.sum(emb * emb, axis=1, keepdims=True) + EPS)).astype(jnp.bfloat16)
    packed[...] = (
        jnp.dot(pick, unit, preferred_element_type=jnp.float32)
        .astype(jnp.bfloat16)
        .reshape(n_clus, cap, depth)
    )
    gathered[0, 0] = packed[0]
    label_row = dot_t(
        jnp.broadcast_to((within + 1).astype(jnp.float32), (8, rows)).astype(jnp.bfloat16), pick
    )[:1]
    labels[0] = label_row

    label_copy = {
        d: copy(labels.at[0], labels.at[d], label_sem, d, at_clus[d]) for d in range(1, n_clus)
    }
    row_copy = {
        d: copy(packed.at[d], gathered.at[0, d], row_sem, d, at_clus[d]) for d in range(1, n_clus)
    }
    core_copy = {
        d: copy(gathered.at[0, d], gathered.at[1, d], core_sem, d, at_src[1]) for d in range(n_clus)
    }
    y_copy = {
        d: copy(gathered.at[0, d], gathered.at[2, d], y_sem, d, at_src[2]) for d in range(n_clus)
    }
    diag_copy = {
        d: copy(gathered.at[2, d], gathered.at[3, d], diag_sem, d, at_src[1]) for d in range(n_clus)
    }
    partial_copy = {
        0: copy(partial.at[1], partial_in.at[0], partial_sem, 0, at_src[1]),
        1: copy(partial.at[3], partial_in.at[1], partial_sem, 1, at_src[1]),
        2: copy(partial.at[2], partial_in.at[2], partial_sem, 2, at_src[2]),
    }
    owned_copy = {
        d: copy(owned.at[d], owned_in.at[d], owned_sem, d, at_clus[d]) for d in range(1, n_clus)
    }
    cent_copy = {
        e: copy(cents.at[0], cents.at[e], cent_sem, e, at_src[e]) for e in range(1, n_src)
    }
    shard_copy = {
        e: copy(shard_labels.at[0], shard_labels.at[e], shard_sem, e, at_src[e])
        for e in range(1, n_src)
    }
    max_copy = {
        d: copy(maxima.at[0], maxima.at[d], max_sem, d, at_clus[d]) for d in range(1, n_clus)
    }

    pl.semaphore_wait(barrier, len(others))
    half = n_clus // 2
    turns = list(range(1, n_clus))
    sends = [d for near in range(half) for d in (near + 1, half + near)]
    sends = [d for i, d in enumerate(sends) if d not in sends[:i]]
    for d in turns:
        label_copy[d].start()
    y_copy[0].start()
    for d in sends:
        row_copy[d].start()
    core_copy[0].start()

    order = (
        jnp.bitwise_xor(within // per, src) * (n_clus * per) + distance * per + within % per
    )
    count = n_src * n_clus * per
    members = jnp.where(
        lax.broadcasted_iota(jnp.int32, (count, rows), 0) == order, 2.0, 0.0
    ).astype(jnp.bfloat16)
    sums = jnp.zeros((count, depth), jnp.float32)
    for part in exact_parts(emb * 0.5):
        sums = sums + jnp.dot(members, part, preferred_element_type=jnp.float32)
    partial[...] = sums.reshape(n_src, n_clus * per, depth)
    for e in range(2):
        partial_copy[e].start()

    def send_labels():
        for d in turns:
            label_copy[d].wait_recv()
        own_labels = own_lanes(labels, n_clus, cap)
        shard_labels[0] = own_labels
        for e in range(1, n_src):
            shard_copy[e].start()
        return own_labels

    def pair_sums():
        for e in range(2):
            partial_copy[e].wait_recv()
        partial[2] = partial[2] + partial_in[1]
        partial_copy[2].start()

    def reduce_sums():
        partial_copy[2].wait_recv()
        total = partial[0] + partial_in[0] + partial_in[2]
        for d in range(n_clus):
            owned[d] = total[d * per : (d + 1) * per]
        for d in range(1, n_clus):
            owned_copy[d].start()

    def finish_sums():
        total = owned[0]
        for d in range(1, n_clus):
            owned_copy[d].wait_recv()
            total = total + owned_in[d]
        cents[0] = total * lax.rsqrt(jnp.sum(total * total, axis=1, keepdims=True) + EPS)
        for e in range(1, n_src):
            cent_copy[e].start()

    def column_labels(e):
        other = jnp.transpose(jnp.broadcast_to(shard_labels[e], (128, slots)))
        return jnp.concatenate([other] * (slots // 128), axis=1)

    def shard_maxima(e, other, first=0, last=n_clus):
        count = (last - first) * cap
        scores = dot_t(
            gathered[e, first:last].reshape(count, depth), gathered[0].reshape(slots, depth)
        )
        allowed = other[first * cap : last * cap] == own_labels
        if e == 0:
            allowed = allowed & (
                lax.broadcasted_iota(jnp.int32, (slots, slots), 0)
                != lax.broadcasted_iota(jnp.int32, (slots, slots), 1)
            )
        return jnp.max(jnp.where(allowed, scores, -1.0), axis=0, keepdims=True)

    def pass_on(d):
        y_copy[d].wait_recv()
        diag_copy[d].start()

    waiting = [0]
    for step, d in enumerate(turns):
        row_copy[d].wait_recv()
        y_copy[d].start()
        core_copy[d].start()
        waiting.append(d)
        if step == 0:
            pair_sums()
        if step == 1:
            own_labels = send_labels()
        if step == 3:
            reduce_sums()
        if step >= 2:
            pass_on(waiting.pop(0))
    pass_on(waiting.pop(0))
    best = shard_maxima(0, column_labels(0))
    for e in range(1, n_src):
        shard_copy[e].wait_recv()
    for d in range(n_clus):
        core_copy[d].wait_recv()
    best = jnp.maximum(best, shard_maxima(1, column_labels(1)))
    for d in waiting:
        pass_on(d)
    finish_sums()
    best = jnp.maximum(best, shard_maxima(2, column_labels(2)))
    other = column_labels(3)
    for d in range(half):
        diag_copy[d].wait_recv()
    best = jnp.maximum(best, shard_maxima(3, other, 0, half))
    for d in range(half, n_clus):
        diag_copy[d].wait_recv()
    maxima[0] = jnp.maximum(best, shard_maxima(3, other, half, n_clus))
    for d in turns:
        max_copy[d].start()

    for e in range(1, n_src):
        cent_copy[e].wait_recv()
    for shard in range(n_src):
        cent_ref[shard * per : (shard + 1) * per, :] = cents[src_peer[shard]]
    for d in turns:
        max_copy[d].wait_recv()
    near = jnp.zeros((8, rows), jnp.float32)
    for part in exact_parts(jnp.broadcast_to(own_lanes(maxima, n_clus, cap), (8, slots))):
        near = near + jnp.dot(part, pick, preferred_element_type=jnp.float32)
    near_ref[...] = near[:1]

    for copies in (
        label_copy,
        row_copy,
        core_copy,
        y_copy,
        diag_copy,
        partial_copy,
        shard_copy,
        owned_copy,
        cent_copy,
        max_copy,
    ):
        for started in copies.values():
            started.wait_send()


def one_kernel(n_clus, n_src, embeddings, cluster):
    rows, depth = embeddings.shape
    cap = 2 * rows // n_clus
    slots = n_clus * cap
    per = CLUS_DEV // n_src
    f32, bf16 = jnp.float32, jnp.bfloat16
    vmem = pl.BlockSpec(memory_space=pltpu.VMEM)
    hbm = pl.BlockSpec(memory_space=pltpu.HBM)
    centroids, nearest = pl.pallas_call(
        functools.partial(owner_kernel, n_clus, n_src, cap),
        out_shape=(
            jax.ShapeDtypeStruct((CLUS_DEV, depth), f32),
            jax.ShapeDtypeStruct((1, rows), f32),
        ),
        in_specs=[hbm, hbm],
        out_specs=(vmem, vmem),
        scratch_shapes=[
            pltpu.VMEM((1, rows), jnp.int32),
            pltpu.VMEM((rows, depth), f32),
            pltpu.VMEM((n_clus, cap, depth), bf16),
            pltpu.VMEM((n_src, n_clus, cap, depth), bf16),
            pltpu.VMEM((n_clus, 1, slots), f32),
            pltpu.VMEM((n_src, 1, slots), f32),
            pltpu.VMEM((n_src, n_clus * per, depth), f32),
            pltpu.VMEM((n_src, n_clus * per, depth), f32),
            pltpu.VMEM((n_clus, per, depth), f32),
            pltpu.VMEM((n_clus, per, depth), f32),
            pltpu.VMEM((n_src, per, depth), f32),
            pltpu.VMEM((n_clus, 1, slots), f32),
        ]
        + [
            pltpu.SemaphoreType.DMA((2, count))
            for count in (n_clus, n_clus, n_clus, n_clus, n_clus, n_src, n_src, n_clus, n_src, n_clus)
        ]
        + [pltpu.SemaphoreType.DMA((2,))],
        compiler_params=pltpu.CompilerParams(
            collective_id=0, has_side_effects=True, vmem_limit_bytes=55040 * 1024
        ),
        cost_estimate=pl.CostEstimate(
            flops=2 * slots * slots * n_src * depth, bytes_accessed=rows * depth * 4, transcendentals=0
        ),
    )(cluster.reshape(1, rows), embeddings)
    return centroids, nearest.reshape(rows)


def block_maxima(current, own_unit, own_labels, own_global, other_unit, other_labels, other_global):
    scores = lax.dot_general(
        own_unit, other_unit, (((1,), (1,)), ((), ())), preferred_element_type=jnp.float32
    )
    allowed = (
        (own_labels[:, None] == other_labels[None, :])
        & (own_global[:, None] != other_global[None, :])
        & (own_labels[:, None] >= 0)
    )
    return jnp.maximum(current, jnp.max(jnp.where(allowed, scores, jnp.float32(-1.0)), axis=1))


def unit_rows(values):
    return (values * lax.rsqrt(jnp.sum(values * values, axis=1, keepdims=True) + 1e-06)).astype(
        jnp.bfloat16
    )


def normalized(owned):
    return owned * lax.rsqrt(jnp.sum(owned * owned, axis=1, keepdims=True) + 1e-06)


def on_device(embeddings, cluster):
    row_count = embeddings.shape[0]
    feature_dim = embeddings.shape[1]
    clus_count = lax.axis_size("clus")
    source_count = lax.axis_size("src")
    capacity = max(2, 2 * row_count // clus_count)
    slot_total = clus_count * capacity
    owner = cluster // CLUS_DEV
    member_hits = (owner[:, None] == jnp.arange(clus_count, dtype=jnp.int32)[None, :]).astype(
        jnp.int32
    )
    running = jnp.cumsum(member_hits, axis=0)
    position = jnp.sum(member_hits * running, axis=1) - 1
    slot_index = owner * capacity + position
    device_number = lax.axis_index("clus") * source_count + lax.axis_index("src")
    global_row = device_number * row_count + jnp.arange(row_count, dtype=jnp.int32)
    send_labels = jnp.full((slot_total,), -1, jnp.int32).at[slot_index].set(cluster)
    send_global = jnp.full((slot_total,), -1, jnp.int32).at[slot_index].set(global_row)
    count = lax.axis_size("clus") * CLUS_DEV
    inside = (cluster >= 0) & (cluster < count)
    segment = jnp.where(inside, cluster, count)
    owned = lax.psum_scatter(
        jax.ops.segment_sum(embeddings, segment, num_segments=count + 1)[:count],
        "clus",
        scatter_dimension=0,
        tiled=True,
    )
    owned = lax.psum(owned, "src")
    centroids = normalized(owned)
    unit = unit_rows(embeddings)
    send_unit = jnp.zeros((slot_total, feature_dim), jnp.bfloat16).at[slot_index].set(unit)
    received, recv_labels, recv_global = (
        lax.all_to_all(send_unit, "clus", split_axis=0, concat_axis=0, tiled=True),
        lax.all_to_all(send_labels, "clus", split_axis=0, concat_axis=0, tiled=True),
        lax.all_to_all(send_global, "clus", split_axis=0, concat_axis=0, tiled=True),
    )
    initial = jnp.full((slot_total,), -1.0, jnp.float32)
    piece_unit = lax.all_gather(received, "src", axis=0, tiled=True)
    piece_labels = lax.all_gather(recv_labels, "src", axis=0, tiled=True)
    piece_global = lax.all_gather(recv_global, "src", axis=0, tiled=True)
    length = piece_unit.shape[0]
    stacked = (
        piece_unit.reshape(length // slot_total, slot_total, feature_dim),
        piece_labels.reshape(length // slot_total, slot_total),
        piece_global.reshape(length // slot_total, slot_total),
    )

    def stepper(carried, sliced):
        return (
            block_maxima(
                carried, received, recv_labels, recv_global, sliced[0], sliced[1], sliced[2]
            ),
            None,
        )

    result, unused = lax.scan(stepper, initial, stacked)
    returned = lax.all_to_all(result, "clus", split_axis=0, concat_axis=0, tiled=True)
    nearest = returned[slot_index]
    return (centroids, nearest)


def fits_one_kernel(n_clus, n_src, rows):
    cap = 2 * rows // n_clus
    return (
        n_src == 4
        and n_clus & (n_clus - 1) == 0
        and cap % 16 == 0
        and n_clus * cap % 128 == 0
        and rows % 128 == 0
    )


def solution(mesh):
    n_clus, n_src = mesh.shape["clus"], mesh.shape["src"]

    def body(embeddings, cluster):
        if fits_one_kernel(n_clus, n_src, embeddings.shape[0]):
            return one_kernel(n_clus, n_src, embeddings, cluster)
        return on_device(embeddings, cluster)

    placed = (P(("clus", "src"), None), P(("clus", "src")))
    return jax.shard_map(
        body,
        mesh=mesh,
        in_specs=placed,
        out_specs=(P("clus", None), P(("clus", "src"))),
        check_vma=False,
    )
```

```python
import functools

import jax
import jax.numpy as jnp
from jax import lax
from jax.experimental import pallas as pl
from jax.experimental.pallas import tpu as pltpu
from jax.sharding import PartitionSpec as P

CLUS_DEV = 8
MESH = pl.DeviceIdType.MESH
EPS = 1e-06
LOADS = 4


def partner(index, distance, count):
    total = 0
    bit = 1
    while bit < count:
        value = (index // bit) % 2
        total = total + bit * ((1 - value) if (distance // bit) % 2 else value)
        bit *= 2
    return total


def exact_parts(values):
    high = values.astype(jnp.bfloat16)
    rest = values - high.astype(jnp.float32)
    middle = rest.astype(jnp.bfloat16)
    low = (rest - middle.astype(jnp.float32)).astype(jnp.bfloat16)
    return high, middle, low


def dot_t(left, right):
    return lax.dot_general(left, right, (((1,), (1,)), ((), ())), preferred_element_type=jnp.float32)


def own_lanes(rows_ref, n_clus, cap):
    width = n_clus * cap
    group = lax.broadcasted_iota(jnp.int32, (1, width), 1) // cap
    total = jnp.zeros((1, width), jnp.float32)
    for d in range(n_clus):
        total = jnp.where(group == d, rows_ref[d], total)
    return total


def owner_kernel(
    n_clus,
    n_src,
    cap,
    cluster_hbm,
    emb_hbm,
    cent_ref,
    near_ref,
    cluster_ref,
    emb_ref,
    packed,
    gathered,
    labels,
    shard_labels,
    partial,
    partial_in,
    owned,
    owned_in,
    cents,
    maxima,
    row_sem,
    y_sem,
    core_sem,
    diag_sem,
    label_sem,
    shard_sem,
    partial_sem,
    owned_sem,
    cent_sem,
    max_sem,
    load_sem,
):
    rows, depth = emb_ref.shape
    slots = n_clus * cap
    per = CLUS_DEV // n_src
    me = lax.axis_index("clus")
    src = lax.axis_index("src")
    clus_peer = [partner(me, d, n_clus) for d in range(n_clus)]
    src_peer = [partner(src, e, n_src) for e in range(n_src)]
    at_clus = [(clus_peer[d], src) for d in range(n_clus)]
    at_src = [(me, src_peer[e]) for e in range(n_src)]

    def copy(source, target, sems, slot, device):
        return pltpu.make_async_remote_copy(
            src_ref=source,
            dst_ref=target,
            send_sem=sems.at[0, slot],
            recv_sem=sems.at[1, slot],
            device_id=device,
            device_id_type=MESH,
        )

    load_cluster = pltpu.make_async_copy(cluster_hbm, cluster_ref, load_sem.at[0])
    band = rows // LOADS
    load_rows = [
        pltpu.make_async_copy(
            emb_hbm.at[pl.ds(i * band, band)], emb_ref.at[pl.ds(i * band, band)], load_sem.at[1 + i]
        )
        for i in range(LOADS)
    ]
    load_cluster.start()
    for load in load_rows:
        load.start()
    barrier = pltpu.get_barrier_semaphore()
    others = [at_clus[d] for d in range(1, n_clus)] + [at_src[e] for e in range(1, n_src)]
    for device in others:
        pl.semaphore_signal(barrier, inc=1, device_id=device, device_id_type=MESH)

    load_cluster.wait()
    cluster = cluster_ref[...]
    within = cluster % CLUS_DEV
    distance = jnp.bitwise_xor(cluster // CLUS_DEV, me)
    hits = lax.broadcasted_iota(jnp.int32, (n_clus, rows), 0) == distance
    earlier = lax.broadcasted_iota(jnp.int32, (rows, rows), 0) < lax.broadcasted_iota(
        jnp.int32, (rows, rows), 1
    )
    before = jnp.dot(
        jnp.where(hits, 1.0, 0.0).astype(jnp.bfloat16),
        jnp.where(earlier, 1.0, 0.0).astype(jnp.bfloat16),
        preferred_element_type=jnp.float32,
    )
    place = jnp.sum(jnp.where(hits, before, 0.0), axis=0, keepdims=True).astype(jnp.int32)
    slot = distance * cap + place
    pick = jnp.where(lax.broadcasted_iota(jnp.int32, (slots, rows), 0) == slot, 1.0, 0.0).astype(
        jnp.bfloat16
    )

    units = []
    for i, load in enumerate(load_rows):
        load.wait()
        part = emb_ref[i * band : (i + 1) * band]
        norm = lax.rsqrt(jnp.sum(part * part, axis=1, keepdims=True) + EPS)
        units.append((part * norm).astype(jnp.bfloat16))
    unit = jnp.concatenate(units, axis=0)
    packed[...] = (
        jnp.dot(pick, unit, preferred_element_type=jnp.float32)
        .astype(jnp.bfloat16)
        .reshape(n_clus, cap, depth)
    )
    gathered[0, 0] = packed[0]
    label_row = dot_t(
        jnp.broadcast_to((within + 1).astype(jnp.float32), (8, rows)).astype(jnp.bfloat16), pick
    )[:1]
    labels[0] = label_row

    label_copy = {
        d: copy(labels.at[0], labels.at[d], label_sem, d, at_clus[d]) for d in range(1, n_clus)
    }
    row_copy = {
        d: copy(packed.at[d], gathered.at[0, d], row_sem, d, at_clus[d]) for d in range(1, n_clus)
    }
    core_copy = {
        d: copy(gathered.at[0, d], gathered.at[1, d], core_sem, d, at_src[1]) for d in range(n_clus)
    }
    y_copy = {
        d: copy(gathered.at[0, d], gathered.at[2, d], y_sem, d, at_src[2]) for d in range(n_clus)
    }
    diag_copy = {
        d: copy(gathered.at[2, d], gathered.at[3, d], diag_sem, d, at_src[1]) for d in range(n_clus)
    }
    partial_copy = {
        0: copy(partial.at[1], partial_in.at[0], partial_sem, 0, at_src[1]),
        1: copy(partial.at[3], partial_in.at[1], partial_sem, 1, at_src[1]),
        2: copy(partial.at[2], partial_in.at[2], partial_sem, 2, at_src[2]),
    }
    owned_copy = {
        d: copy(owned.at[d], owned_in.at[d], owned_sem, d, at_clus[d]) for d in range(1, n_clus)
    }
    cent_copy = {
        e: copy(cents.at[0], cents.at[e], cent_sem, e, at_src[e]) for e in range(1, n_src)
    }
    shard_copy = {
        e: copy(shard_labels.at[0], shard_labels.at[e], shard_sem, e, at_src[e])
        for e in range(1, n_src)
    }
    max_copy = {
        d: copy(maxima.at[0], maxima.at[d], max_sem, d, at_clus[d]) for d in range(1, n_clus)
    }

    pl.semaphore_wait(barrier, len(others))
    half = n_clus // 2
    turns = list(range(1, n_clus))
    sends = [d for near in range(half) for d in (near + 1, half + near)]
    sends = [d for i, d in enumerate(sends) if d not in sends[:i]]
    for d in turns:
        label_copy[d].start()
    y_copy[0].start()
    for d in sends:
        row_copy[d].start()
    core_copy[0].start()

    order = (
        jnp.bitwise_xor(within // per, src) * (n_clus * per) + distance * per + within % per
    )
    count = n_src * n_clus * per
    members = jnp.where(
        lax.broadcasted_iota(jnp.int32, (count, rows), 0) == order, 2.0, 0.0
    ).astype(jnp.bfloat16)
    sums = jnp.zeros((count, depth), jnp.float32)
    for part in exact_parts(emb_ref[...] * 0.5):
        sums = sums + jnp.dot(members, part, preferred_element_type=jnp.float32)
    partial[...] = sums.reshape(n_src, n_clus * per, depth)
    for e in range(2):
        partial_copy[e].start()

    def send_labels():
        for d in turns:
            label_copy[d].wait_recv()
        own_labels = own_lanes(labels, n_clus, cap)
        shard_labels[0] = own_labels
        for e in range(1, n_src):
            shard_copy[e].start()
        return own_labels

    def pair_sums():
        for e in range(2):
            partial_copy[e].wait_recv()
        partial[2] = partial[2] + partial_in[1]
        partial_copy[2].start()

    def reduce_sums():
        partial_copy[2].wait_recv()
        total = partial[0] + partial_in[0] + partial_in[2]
        for d in range(n_clus):
            owned[d] = total[d * per : (d + 1) * per]
        for d in range(1, n_clus):
            owned_copy[d].start()

    def finish_sums():
        total = owned[0]
        for d in range(1, n_clus):
            owned_copy[d].wait_recv()
            total = total + owned_in[d]
        cents[0] = total * lax.rsqrt(jnp.sum(total * total, axis=1, keepdims=True) + EPS)
        for e in range(1, n_src):
            cent_copy[e].start()

    def column_labels(e):
        other = jnp.transpose(jnp.broadcast_to(shard_labels[e], (128, slots)))
        return jnp.concatenate([other] * (slots // 128), axis=1)

    def shard_maxima(e, other, first=0, last=n_clus):
        count = (last - first) * cap
        scores = dot_t(
            gathered[e, first:last].reshape(count, depth), gathered[0].reshape(slots, depth)
        )
        allowed = other[first * cap : last * cap] == own_labels
        if e == 0:
            allowed = allowed & (
                lax.broadcasted_iota(jnp.int32, (slots, slots), 0)
                != lax.broadcasted_iota(jnp.int32, (slots, slots), 1)
            )
        return jnp.max(jnp.where(allowed, scores, -1.0), axis=0, keepdims=True)

    def pass_on(d):
        y_copy[d].wait_recv()
        diag_copy[d].start()

    waiting = [0]
    for step, d in enumerate(turns):
        row_copy[d].wait_recv()
        y_copy[d].start()
        core_copy[d].start()
        waiting.append(d)
        if step == 0:
            pair_sums()
        if step == 1:
            own_labels = send_labels()
        if step == 3:
            reduce_sums()
        if 2 <= step < len(turns) - 1:
            pass_on(waiting.pop(0))
    best = shard_maxima(0, column_labels(0))
    for e in range(1, n_src):
        shard_copy[e].wait_recv()
    for d in range(n_clus):
        core_copy[d].wait_recv()
    best = jnp.maximum(best, shard_maxima(1, column_labels(1)))
    last = waiting.pop()
    for d in waiting:
        pass_on(d)
    finish_sums()
    over_y = column_labels(2)
    best = jnp.maximum(best, shard_maxima(2, over_y, 0, half))
    across = column_labels(3)
    for d in range(half):
        diag_copy[d].wait_recv()
    best = jnp.maximum(best, shard_maxima(3, across, 0, half))
    pass_on(last)
    best = jnp.maximum(best, shard_maxima(2, over_y, half, n_clus))
    for d in range(half, n_clus):
        diag_copy[d].wait_recv()
    maxima[0] = jnp.maximum(best, shard_maxima(3, across, half, n_clus))
    for d in turns:
        max_copy[d].start()

    for e in range(1, n_src):
        cent_copy[e].wait_recv()
    for shard in range(n_src):
        cent_ref[shard * per : (shard + 1) * per, :] = cents[src_peer[shard]]
    for d in turns:
        max_copy[d].wait_recv()
    near = jnp.zeros((8, rows), jnp.float32)
    for part in exact_parts(jnp.broadcast_to(own_lanes(maxima, n_clus, cap), (8, slots))):
        near = near + jnp.dot(part, pick, preferred_element_type=jnp.float32)
    near_ref[...] = near[:1]

    for copies in (
        label_copy,
        row_copy,
        core_copy,
        y_copy,
        diag_copy,
        partial_copy,
        shard_copy,
        owned_copy,
        cent_copy,
        max_copy,
    ):
        for started in copies.values():
            started.wait_send()


def one_kernel(n_clus, n_src, embeddings, cluster):
    rows, depth = embeddings.shape
    cap = 2 * rows // n_clus
    slots = n_clus * cap
    per = CLUS_DEV // n_src
    f32, bf16 = jnp.float32, jnp.bfloat16
    vmem = pl.BlockSpec(memory_space=pltpu.VMEM)
    hbm = pl.BlockSpec(memory_space=pltpu.HBM)
    centroids, nearest = pl.pallas_call(
        functools.partial(owner_kernel, n_clus, n_src, cap),
        out_shape=(
            jax.ShapeDtypeStruct((CLUS_DEV, depth), f32),
            jax.ShapeDtypeStruct((1, rows), f32),
        ),
        in_specs=[hbm, hbm],
        out_specs=(vmem, vmem),
        scratch_shapes=[
            pltpu.VMEM((1, rows), jnp.int32),
            pltpu.VMEM((rows, depth), f32),
            pltpu.VMEM((n_clus, cap, depth), bf16),
            pltpu.VMEM((n_src, n_clus, cap, depth), bf16),
            pltpu.VMEM((n_clus, 1, slots), f32),
            pltpu.VMEM((n_src, 1, slots), f32),
            pltpu.VMEM((n_src, n_clus * per, depth), f32),
            pltpu.VMEM((n_src, n_clus * per, depth), f32),
            pltpu.VMEM((n_clus, per, depth), f32),
            pltpu.VMEM((n_clus, per, depth), f32),
            pltpu.VMEM((n_src, per, depth), f32),
            pltpu.VMEM((n_clus, 1, slots), f32),
        ]
        + [
            pltpu.SemaphoreType.DMA((2, count))
            for count in (n_clus, n_clus, n_clus, n_clus, n_clus, n_src, n_src, n_clus, n_src, n_clus)
        ]
        + [pltpu.SemaphoreType.DMA((1 + LOADS,))],
        compiler_params=pltpu.CompilerParams(
            collective_id=0, has_side_effects=True, vmem_limit_bytes=32 * 1024 * 1024
        ),
        cost_estimate=pl.CostEstimate(
            flops=2 * slots * slots * n_src * depth, bytes_accessed=rows * depth * 4, transcendentals=0
        ),
    )(
        pltpu.with_memory_space_constraint(cluster.reshape(1, rows), pltpu.HBM),
        pltpu.with_memory_space_constraint(embeddings, pltpu.HBM),
    )
    return centroids, nearest.reshape(rows)


def block_maxima(current, own_unit, own_labels, own_global, other_unit, other_labels, other_global):
    scores = lax.dot_general(
        own_unit, other_unit, (((1,), (1,)), ((), ())), preferred_element_type=jnp.float32
    )
    allowed = (
        (own_labels[:, None] == other_labels[None, :])
        & (own_global[:, None] != other_global[None, :])
        & (own_labels[:, None] >= 0)
    )
    return jnp.maximum(current, jnp.max(jnp.where(allowed, scores, jnp.float32(-1.0)), axis=1))


def unit_rows(values):
    return (values * lax.rsqrt(jnp.sum(values * values, axis=1, keepdims=True) + 1e-06)).astype(
        jnp.bfloat16
    )


def normalized(owned):
    return owned * lax.rsqrt(jnp.sum(owned * owned, axis=1, keepdims=True) + 1e-06)


def on_device(embeddings, cluster):
    row_count = embeddings.shape[0]
    feature_dim = embeddings.shape[1]
    clus_count = lax.axis_size("clus")
    source_count = lax.axis_size("src")
    capacity = max(2, 2 * row_count // clus_count)
    slot_total = clus_count * capacity
    owner = cluster // CLUS_DEV
    member_hits = (owner[:, None] == jnp.arange(clus_count, dtype=jnp.int32)[None, :]).astype(
        jnp.int32
    )
    running = jnp.cumsum(member_hits, axis=0)
    position = jnp.sum(member_hits * running, axis=1) - 1
    slot_index = owner * capacity + position
    device_number = lax.axis_index("clus") * source_count + lax.axis_index("src")
    global_row = device_number * row_count + jnp.arange(row_count, dtype=jnp.int32)
    send_labels = jnp.full((slot_total,), -1, jnp.int32).at[slot_index].set(cluster)
    send_global = jnp.full((slot_total,), -1, jnp.int32).at[slot_index].set(global_row)
    count = lax.axis_size("clus") * CLUS_DEV
    inside = (cluster >= 0) & (cluster < count)
    segment = jnp.where(inside, cluster, count)
    owned = lax.psum_scatter(
        jax.ops.segment_sum(embeddings, segment, num_segments=count + 1)[:count],
        "clus",
        scatter_dimension=0,
        tiled=True,
    )
    owned = lax.psum(owned, "src")
    centroids = normalized(owned)
    unit = unit_rows(embeddings)
    send_unit = jnp.zeros((slot_total, feature_dim), jnp.bfloat16).at[slot_index].set(unit)
    received, recv_labels, recv_global = (
        lax.all_to_all(send_unit, "clus", split_axis=0, concat_axis=0, tiled=True),
        lax.all_to_all(send_labels, "clus", split_axis=0, concat_axis=0, tiled=True),
        lax.all_to_all(send_global, "clus", split_axis=0, concat_axis=0, tiled=True),
    )
    initial = jnp.full((slot_total,), -1.0, jnp.float32)
    piece_unit = lax.all_gather(received, "src", axis=0, tiled=True)
    piece_labels = lax.all_gather(recv_labels, "src", axis=0, tiled=True)
    piece_global = lax.all_gather(recv_global, "src", axis=0, tiled=True)
    length = piece_unit.shape[0]
    stacked = (
        piece_unit.reshape(length // slot_total, slot_total, feature_dim),
        piece_labels.reshape(length // slot_total, slot_total),
        piece_global.reshape(length // slot_total, slot_total),
    )

    def stepper(carried, sliced):
        return (
            block_maxima(
                carried, received, recv_labels, recv_global, sliced[0], sliced[1], sliced[2]
            ),
            None,
        )

    result, unused = lax.scan(stepper, initial, stacked)
    returned = lax.all_to_all(result, "clus", split_axis=0, concat_axis=0, tiled=True)
    nearest = returned[slot_index]
    return (centroids, nearest)


def fits_one_kernel(n_clus, n_src, rows):
    cap = 2 * rows // n_clus
    return (
        n_src == 4
        and n_clus & (n_clus - 1) == 0
        and cap % 16 == 0
        and n_clus * cap % 128 == 0
        and rows % 128 == 0
    )


def solution(mesh):
    n_clus, n_src = mesh.shape["clus"], mesh.shape["src"]

    def body(embeddings, cluster):
        if fits_one_kernel(n_clus, n_src, embeddings.shape[0]):
            return one_kernel(n_clus, n_src, embeddings, cluster)
        return on_device(embeddings, cluster)

    placed = (P(("clus", "src"), None), P(("clus", "src")))
    return jax.shard_map(
        body,
        mesh=mesh,
        in_specs=placed,
        out_specs=(P("clus", None), P(("clus", "src"))),
        check_vma=False,
    )
```

```python
import functools

import jax
import jax.numpy as jnp
from jax import lax
from jax.experimental import pallas as pl
from jax.experimental.pallas import tpu as pltpu
from jax.sharding import PartitionSpec as P

CLUS_DEV = 8
MESH = pl.DeviceIdType.MESH
EPS = 1e-06
LOADS = 4


def partner(index, distance, count):
    total = 0
    bit = 1
    while bit < count:
        value = (index // bit) % 2
        total = total + bit * ((1 - value) if (distance // bit) % 2 else value)
        bit *= 2
    return total


def exact_parts(values):
    high = values.astype(jnp.bfloat16)
    rest = values - high.astype(jnp.float32)
    middle = rest.astype(jnp.bfloat16)
    low = (rest - middle.astype(jnp.float32)).astype(jnp.bfloat16)
    return high, middle, low


def dot_t(left, right):
    return lax.dot_general(left, right, (((1,), (1,)), ((), ())), preferred_element_type=jnp.float32)


def own_lanes(rows_ref, n_clus, cap):
    width = n_clus * cap
    group = lax.broadcasted_iota(jnp.int32, (1, width), 1) // cap
    total = jnp.zeros((1, width), jnp.float32)
    for d in range(n_clus):
        total = jnp.where(group == d, rows_ref[d], total)
    return total


def owner_kernel(
    n_clus,
    n_src,
    cap,
    cluster_hbm,
    emb_hbm,
    cent_ref,
    near_ref,
    cluster_ref,
    emb_ref,
    packed,
    gathered,
    labels,
    shard_labels,
    partial,
    partial_in,
    owned,
    owned_in,
    cents,
    maxima,
    row_sem,
    y_sem,
    core_sem,
    diag_sem,
    label_sem,
    shard_sem,
    partial_sem,
    owned_sem,
    cent_sem,
    max_sem,
    load_sem,
):
    rows, depth = emb_ref.shape
    slots = n_clus * cap
    per = CLUS_DEV // n_src
    me = lax.axis_index("clus")
    src = lax.axis_index("src")
    clus_peer = [partner(me, d, n_clus) for d in range(n_clus)]
    src_peer = [partner(src, e, n_src) for e in range(n_src)]
    at_clus = [(clus_peer[d], src) for d in range(n_clus)]
    at_src = [(me, src_peer[e]) for e in range(n_src)]

    def copy(source, target, sems, slot, device):
        return pltpu.make_async_remote_copy(
            src_ref=source,
            dst_ref=target,
            send_sem=sems.at[0, slot],
            recv_sem=sems.at[1, slot],
            device_id=device,
            device_id_type=MESH,
        )

    load_cluster = pltpu.make_async_copy(cluster_hbm, cluster_ref, load_sem.at[0])
    band = rows // LOADS
    load_rows = [
        pltpu.make_async_copy(
            emb_hbm.at[pl.ds(i * band, band)], emb_ref.at[pl.ds(i * band, band)], load_sem.at[1 + i]
        )
        for i in range(LOADS)
    ]
    load_cluster.start()
    for load in load_rows:
        load.start()
    barrier = pltpu.get_barrier_semaphore()
    others = [at_clus[d] for d in range(1, n_clus)] + [at_src[e] for e in range(1, n_src)]
    for device in others:
        pl.semaphore_signal(barrier, inc=1, device_id=device, device_id_type=MESH)

    load_cluster.wait()
    cluster = cluster_ref[...]
    within = cluster % CLUS_DEV
    distance = jnp.bitwise_xor(cluster // CLUS_DEV, me)
    hits = lax.broadcasted_iota(jnp.int32, (n_clus, rows), 0) == distance
    earlier = lax.broadcasted_iota(jnp.int32, (rows, rows), 0) < lax.broadcasted_iota(
        jnp.int32, (rows, rows), 1
    )
    before = jnp.dot(
        jnp.where(hits, 1.0, 0.0).astype(jnp.bfloat16),
        jnp.where(earlier, 1.0, 0.0).astype(jnp.bfloat16),
        preferred_element_type=jnp.float32,
    )
    place = jnp.sum(jnp.where(hits, before, 0.0), axis=0, keepdims=True).astype(jnp.int32)
    slot = distance * cap + place
    pick = jnp.where(lax.broadcasted_iota(jnp.int32, (slots, rows), 0) == slot, 1.0, 0.0).astype(
        jnp.bfloat16
    )

    units = []
    for i, load in enumerate(load_rows):
        load.wait()
        part = emb_ref[i * band : (i + 1) * band]
        norm = lax.rsqrt(jnp.sum(part * part, axis=1, keepdims=True) + EPS)
        units.append((part * norm).astype(jnp.bfloat16))
    unit = jnp.concatenate(units, axis=0)
    packed[...] = (
        jnp.dot(pick, unit, preferred_element_type=jnp.float32)
        .astype(jnp.bfloat16)
        .reshape(n_clus, cap, depth)
    )
    gathered[0, 0] = packed[0]
    label_row = dot_t(
        jnp.broadcast_to((within + 1).astype(jnp.float32), (8, rows)).astype(jnp.bfloat16), pick
    )[:1]
    labels[0] = label_row

    label_copy = {
        d: copy(labels.at[0], labels.at[d], label_sem, d, at_clus[d]) for d in range(1, n_clus)
    }
    row_copy = {
        d: copy(packed.at[d], gathered.at[0, d], row_sem, d, at_clus[d]) for d in range(1, n_clus)
    }
    core_copy = {
        d: copy(gathered.at[0, d], gathered.at[1, d], core_sem, d, at_src[1]) for d in range(n_clus)
    }
    y_copy = {
        d: copy(gathered.at[0, d], gathered.at[2, d], y_sem, d, at_src[2]) for d in range(n_clus)
    }
    diag_copy = {
        d: copy(gathered.at[2, d], gathered.at[3, d], diag_sem, d, at_src[1]) for d in range(n_clus)
    }
    partial_copy = {
        0: copy(partial.at[1], partial_in.at[0], partial_sem, 0, at_src[1]),
        1: copy(partial.at[3], partial_in.at[1], partial_sem, 1, at_src[1]),
        2: copy(partial.at[2], partial_in.at[2], partial_sem, 2, at_src[2]),
    }
    owned_copy = {
        d: copy(owned.at[d], owned_in.at[d], owned_sem, d, at_clus[d]) for d in range(1, n_clus)
    }
    cent_copy = {
        e: copy(cents.at[0], cents.at[e], cent_sem, e, at_src[e]) for e in range(1, n_src)
    }
    shard_copy = {
        e: copy(shard_labels.at[0], shard_labels.at[e], shard_sem, e, at_src[e])
        for e in range(1, n_src)
    }
    max_copy = {
        d: copy(maxima.at[0], maxima.at[d], max_sem, d, at_clus[d]) for d in range(1, n_clus)
    }

    pl.semaphore_wait(barrier, len(others))
    half = n_clus // 2
    turns = list(range(1, n_clus))
    follows = {turns[0]: half + 1}
    follows.update({d: d + 2 for d in range(half, n_clus - 2)})
    for d in turns:
        label_copy[d].start()
    y_copy[0].start()
    for d in range(1, half + 1):
        row_copy[d].start()
    core_copy[0].start()

    order = (
        jnp.bitwise_xor(within // per, src) * (n_clus * per) + distance * per + within % per
    )
    count = n_src * n_clus * per
    members = jnp.where(
        lax.broadcasted_iota(jnp.int32, (count, rows), 0) == order, 2.0, 0.0
    ).astype(jnp.bfloat16)
    sums = jnp.zeros((count, depth), jnp.float32)
    for part in exact_parts(emb_ref[...] * 0.5):
        sums = sums + jnp.dot(members, part, preferred_element_type=jnp.float32)
    partial[...] = sums.reshape(n_src, n_clus * per, depth)
    for e in range(2):
        partial_copy[e].start()

    def send_labels():
        for d in turns:
            label_copy[d].wait_recv()
        own_labels = own_lanes(labels, n_clus, cap)
        shard_labels[0] = own_labels
        for e in range(1, n_src):
            shard_copy[e].start()
        return own_labels

    def pair_sums():
        for e in range(2):
            partial_copy[e].wait_recv()
        partial[2] = partial[2] + partial_in[1]
        partial_copy[2].start()

    def reduce_sums():
        partial_copy[2].wait_recv()
        total = partial[0] + partial_in[0] + partial_in[2]
        for d in range(n_clus):
            owned[d] = total[d * per : (d + 1) * per]
        for d in range(1, n_clus):
            owned_copy[d].start()

    def finish_sums():
        total = owned[0]
        for d in range(1, n_clus):
            owned_copy[d].wait_recv()
            total = total + owned_in[d]
        cents[0] = total * lax.rsqrt(jnp.sum(total * total, axis=1, keepdims=True) + EPS)
        for e in range(1, n_src):
            cent_copy[e].start()

    def column_labels(e):
        other = jnp.transpose(jnp.broadcast_to(shard_labels[e], (128, slots)))
        return jnp.concatenate([other] * (slots // 128), axis=1)

    def shard_maxima(e, other, first=0, last=n_clus):
        count = (last - first) * cap
        scores = dot_t(
            gathered[e, first:last].reshape(count, depth), gathered[0].reshape(slots, depth)
        )
        allowed = other[first * cap : last * cap] == own_labels
        if e == 0:
            allowed = allowed & (
                lax.broadcasted_iota(jnp.int32, (slots, slots), 0)
                != lax.broadcasted_iota(jnp.int32, (slots, slots), 1)
            )
        return jnp.max(jnp.where(allowed, scores, -1.0), axis=0, keepdims=True)

    def pass_on(d):
        y_copy[d].wait_recv()
        diag_copy[d].start()

    waiting = [0]
    for step, d in enumerate(turns):
        row_copy[d].wait_recv()
        if d in follows:
            row_copy[follows[d]].start()
        y_copy[d].start()
        core_copy[d].start()
        waiting.append(d)
        if step == 0:
            pair_sums()
        if step == 1:
            own_labels = send_labels()
        if step == 3:
            reduce_sums()
        if 2 <= step < len(turns) - 1:
            pass_on(waiting.pop(0))
    best = shard_maxima(0, column_labels(0))
    for e in range(1, n_src):
        shard_copy[e].wait_recv()
    for d in range(n_clus):
        core_copy[d].wait_recv()
    best = jnp.maximum(best, shard_maxima(1, column_labels(1)))
    last = waiting.pop()
    for d in waiting:
        pass_on(d)
    finish_sums()
    over_y = column_labels(2)
    best = jnp.maximum(best, shard_maxima(2, over_y, 0, half))
    across = column_labels(3)
    for d in range(half):
        diag_copy[d].wait_recv()
    best = jnp.maximum(best, shard_maxima(3, across, 0, half))
    pass_on(last)
    best = jnp.maximum(best, shard_maxima(2, over_y, half, n_clus))
    for d in range(half, n_clus):
        diag_copy[d].wait_recv()
    maxima[0] = jnp.maximum(best, shard_maxima(3, across, half, n_clus))
    for d in turns:
        max_copy[d].start()

    for e in range(1, n_src):
        cent_copy[e].wait_recv()
    for shard in range(n_src):
        cent_ref[shard * per : (shard + 1) * per, :] = cents[src_peer[shard]]
    for d in turns:
        max_copy[d].wait_recv()
    near = jnp.zeros((8, rows), jnp.float32)
    for part in exact_parts(jnp.broadcast_to(own_lanes(maxima, n_clus, cap), (8, slots))):
        near = near + jnp.dot(part, pick, preferred_element_type=jnp.float32)
    near_ref[...] = near[:1]

    for copies in (
        label_copy,
        row_copy,
        core_copy,
        y_copy,
        diag_copy,
        partial_copy,
        shard_copy,
        owned_copy,
        cent_copy,
        max_copy,
    ):
        for started in copies.values():
            started.wait_send()


def one_kernel(n_clus, n_src, embeddings, cluster):
    rows, depth = embeddings.shape
    cap = 2 * rows // n_clus
    slots = n_clus * cap
    per = CLUS_DEV // n_src
    f32, bf16 = jnp.float32, jnp.bfloat16
    vmem = pl.BlockSpec(memory_space=pltpu.VMEM)
    hbm = pl.BlockSpec(memory_space=pltpu.HBM)
    centroids, nearest = pl.pallas_call(
        functools.partial(owner_kernel, n_clus, n_src, cap),
        out_shape=(
            jax.ShapeDtypeStruct((CLUS_DEV, depth), f32),
            jax.ShapeDtypeStruct((1, rows), f32),
        ),
        in_specs=[hbm, hbm],
        out_specs=(vmem, vmem),
        scratch_shapes=[
            pltpu.VMEM((1, rows), jnp.int32),
            pltpu.VMEM((rows, depth), f32),
            pltpu.VMEM((n_clus, cap, depth), bf16),
            pltpu.VMEM((n_src, n_clus, cap, depth), bf16),
            pltpu.VMEM((n_clus, 1, slots), f32),
            pltpu.VMEM((n_src, 1, slots), f32),
            pltpu.VMEM((n_src, n_clus * per, depth), f32),
            pltpu.VMEM((n_src, n_clus * per, depth), f32),
            pltpu.VMEM((n_clus, per, depth), f32),
            pltpu.VMEM((n_clus, per, depth), f32),
            pltpu.VMEM((n_src, per, depth), f32),
            pltpu.VMEM((n_clus, 1, slots), f32),
        ]
        + [
            pltpu.SemaphoreType.DMA((2, count))
            for count in (n_clus, n_clus, n_clus, n_clus, n_clus, n_src, n_src, n_clus, n_src, n_clus)
        ]
        + [pltpu.SemaphoreType.DMA((1 + LOADS,))],
        compiler_params=pltpu.CompilerParams(
            collective_id=0, has_side_effects=True, vmem_limit_bytes=32 * 1024 * 1024
        ),
        cost_estimate=pl.CostEstimate(
            flops=2 * slots * slots * n_src * depth, bytes_accessed=rows * depth * 4, transcendentals=0
        ),
    )(
        pltpu.with_memory_space_constraint(cluster.reshape(1, rows), pltpu.HBM),
        pltpu.with_memory_space_constraint(embeddings, pltpu.HBM),
    )
    return centroids, nearest.reshape(rows)


def block_maxima(current, own_unit, own_labels, own_global, other_unit, other_labels, other_global):
    scores = lax.dot_general(
        own_unit, other_unit, (((1,), (1,)), ((), ())), preferred_element_type=jnp.float32
    )
    allowed = (
        (own_labels[:, None] == other_labels[None, :])
        & (own_global[:, None] != other_global[None, :])
        & (own_labels[:, None] >= 0)
    )
    return jnp.maximum(current, jnp.max(jnp.where(allowed, scores, jnp.float32(-1.0)), axis=1))


def unit_rows(values):
    return (values * lax.rsqrt(jnp.sum(values * values, axis=1, keepdims=True) + 1e-06)).astype(
        jnp.bfloat16
    )


def normalized(owned):
    return owned * lax.rsqrt(jnp.sum(owned * owned, axis=1, keepdims=True) + 1e-06)


def on_device(embeddings, cluster):
    row_count = embeddings.shape[0]
    feature_dim = embeddings.shape[1]
    clus_count = lax.axis_size("clus")
    source_count = lax.axis_size("src")
    capacity = max(2, 2 * row_count // clus_count)
    slot_total = clus_count * capacity
    owner = cluster // CLUS_DEV
    member_hits = (owner[:, None] == jnp.arange(clus_count, dtype=jnp.int32)[None, :]).astype(
        jnp.int32
    )
    running = jnp.cumsum(member_hits, axis=0)
    position = jnp.sum(member_hits * running, axis=1) - 1
    slot_index = owner * capacity + position
    device_number = lax.axis_index("clus") * source_count + lax.axis_index("src")
    global_row = device_number * row_count + jnp.arange(row_count, dtype=jnp.int32)
    send_labels = jnp.full((slot_total,), -1, jnp.int32).at[slot_index].set(cluster)
    send_global = jnp.full((slot_total,), -1, jnp.int32).at[slot_index].set(global_row)
    count = lax.axis_size("clus") * CLUS_DEV
    inside = (cluster >= 0) & (cluster < count)
    segment = jnp.where(inside, cluster, count)
    owned = lax.psum_scatter(
        jax.ops.segment_sum(embeddings, segment, num_segments=count + 1)[:count],
        "clus",
        scatter_dimension=0,
        tiled=True,
    )
    owned = lax.psum(owned, "src")
    centroids = normalized(owned)
    unit = unit_rows(embeddings)
    send_unit = jnp.zeros((slot_total, feature_dim), jnp.bfloat16).at[slot_index].set(unit)
    received, recv_labels, recv_global = (
        lax.all_to_all(send_unit, "clus", split_axis=0, concat_axis=0, tiled=True),
        lax.all_to_all(send_labels, "clus", split_axis=0, concat_axis=0, tiled=True),
        lax.all_to_all(send_global, "clus", split_axis=0, concat_axis=0, tiled=True),
    )
    initial = jnp.full((slot_total,), -1.0, jnp.float32)
    piece_unit = lax.all_gather(received, "src", axis=0, tiled=True)
    piece_labels = lax.all_gather(recv_labels, "src", axis=0, tiled=True)
    piece_global = lax.all_gather(recv_global, "src", axis=0, tiled=True)
    length = piece_unit.shape[0]
    stacked = (
        piece_unit.reshape(length // slot_total, slot_total, feature_dim),
        piece_labels.reshape(length // slot_total, slot_total),
        piece_global.reshape(length // slot_total, slot_total),
    )

    def stepper(carried, sliced):
        return (
            block_maxima(
                carried, received, recv_labels, recv_global, sliced[0], sliced[1], sliced[2]
            ),
            None,
        )

    result, unused = lax.scan(stepper, initial, stacked)
    returned = lax.all_to_all(result, "clus", split_axis=0, concat_axis=0, tiled=True)
    nearest = returned[slot_index]
    return (centroids, nearest)


def fits_one_kernel(n_clus, n_src, rows):
    cap = 2 * rows // n_clus
    return (
        n_src == 4
        and n_clus & (n_clus - 1) == 0
        and cap % 16 == 0
        and n_clus * cap % 128 == 0
        and rows % 128 == 0
    )


def solution(mesh):
    n_clus, n_src = mesh.shape["clus"], mesh.shape["src"]

    def body(embeddings, cluster):
        if fits_one_kernel(n_clus, n_src, embeddings.shape[0]):
            return one_kernel(n_clus, n_src, embeddings, cluster)
        return on_device(embeddings, cluster)

    placed = (P(("clus", "src"), None), P(("clus", "src")))
    return jax.shard_map(
        body,
        mesh=mesh,
        in_specs=placed,
        out_specs=(P("clus", None), P(("clus", "src"))),
        check_vma=False,
    )
```

```python
import functools

import jax
import jax.numpy as jnp
from jax import lax
from jax.experimental import pallas as pl
from jax.experimental.pallas import tpu as pltpu
from jax.sharding import PartitionSpec as P

CLUS_DEV = 8
MESH = pl.DeviceIdType.MESH
EPS = 1e-06
LOADS = 4


def partner(index, distance, count):
    total = 0
    bit = 1
    while bit < count:
        value = (index // bit) % 2
        total = total + bit * ((1 - value) if (distance // bit) % 2 else value)
        bit *= 2
    return total


def exact_parts(values):
    high = values.astype(jnp.bfloat16)
    rest = values - high.astype(jnp.float32)
    middle = rest.astype(jnp.bfloat16)
    low = (rest - middle.astype(jnp.float32)).astype(jnp.bfloat16)
    return high, middle, low


def dot_t(left, right):
    return lax.dot_general(left, right, (((1,), (1,)), ((), ())), preferred_element_type=jnp.float32)


def own_lanes(rows_ref, n_clus, cap):
    width = n_clus * cap
    group = lax.broadcasted_iota(jnp.int32, (1, width), 1) // cap
    total = jnp.zeros((1, width), jnp.float32)
    for d in range(n_clus):
        total = jnp.where(group == d, rows_ref[d], total)
    return total


def owner_kernel(
    n_clus,
    n_src,
    cap,
    cluster_hbm,
    emb_hbm,
    cent_ref,
    near_ref,
    cluster_ref,
    emb_ref,
    packed,
    gathered,
    labels,
    shard_labels,
    partial,
    partial_in,
    owned,
    owned_in,
    cents,
    maxima,
    row_sem,
    y_sem,
    core_sem,
    diag_sem,
    label_sem,
    shard_sem,
    partial_sem,
    owned_sem,
    cent_sem,
    max_sem,
    load_sem,
):
    rows, depth = emb_ref.shape
    slots = n_clus * cap
    per = CLUS_DEV // n_src
    me = lax.axis_index("clus")
    src = lax.axis_index("src")
    clus_peer = [partner(me, d, n_clus) for d in range(n_clus)]
    src_peer = [partner(src, e, n_src) for e in range(n_src)]
    at_clus = [(clus_peer[d], src) for d in range(n_clus)]
    at_src = [(me, src_peer[e]) for e in range(n_src)]

    def copy(source, target, sems, slot, device):
        return pltpu.make_async_remote_copy(
            src_ref=source,
            dst_ref=target,
            send_sem=sems.at[0, slot],
            recv_sem=sems.at[1, slot],
            device_id=device,
            device_id_type=MESH,
        )

    load_cluster = pltpu.make_async_copy(cluster_hbm, cluster_ref, load_sem.at[0])
    band = rows // LOADS
    load_rows = [
        pltpu.make_async_copy(
            emb_hbm.at[pl.ds(i * band, band)], emb_ref.at[pl.ds(i * band, band)], load_sem.at[1 + i]
        )
        for i in range(LOADS)
    ]
    load_cluster.start()
    for load in load_rows:
        load.start()
    barrier = pltpu.get_barrier_semaphore()
    others = [at_clus[d] for d in range(1, n_clus)] + [at_src[e] for e in range(1, n_src)]
    for device in others:
        pl.semaphore_signal(barrier, inc=1, device_id=device, device_id_type=MESH)

    load_cluster.wait()
    cluster = cluster_ref[...]
    within = cluster % CLUS_DEV
    distance = jnp.bitwise_xor(cluster // CLUS_DEV, me)
    hits = lax.broadcasted_iota(jnp.int32, (n_clus, rows), 0) == distance
    earlier = lax.broadcasted_iota(jnp.int32, (rows, rows), 0) < lax.broadcasted_iota(
        jnp.int32, (rows, rows), 1
    )
    before = jnp.dot(
        jnp.where(hits, 1.0, 0.0).astype(jnp.bfloat16),
        jnp.where(earlier, 1.0, 0.0).astype(jnp.bfloat16),
        preferred_element_type=jnp.float32,
    )
    place = jnp.sum(jnp.where(hits, before, 0.0), axis=0, keepdims=True).astype(jnp.int32)
    slot = distance * cap + place
    pick = jnp.where(lax.broadcasted_iota(jnp.int32, (slots, rows), 0) == slot, 1.0, 0.0).astype(
        jnp.bfloat16
    )

    units = []
    for i, load in enumerate(load_rows):
        load.wait()
        part = emb_ref[i * band : (i + 1) * band]
        norm = lax.rsqrt(jnp.sum(part * part, axis=1, keepdims=True) + EPS)
        units.append((part * norm).astype(jnp.bfloat16))
    unit = jnp.concatenate(units, axis=0)
    packed[...] = (
        jnp.dot(pick, unit, preferred_element_type=jnp.float32)
        .astype(jnp.bfloat16)
        .reshape(n_clus, cap, depth)
    )
    gathered[0, 0] = packed[0]
    label_row = dot_t(
        jnp.broadcast_to((within + 1).astype(jnp.float32), (8, rows)).astype(jnp.bfloat16), pick
    )[:1]
    labels[0] = label_row

    label_copy = {
        d: copy(labels.at[0], labels.at[d], label_sem, d, at_clus[d]) for d in range(1, n_clus)
    }
    row_copy = {
        d: copy(packed.at[d], gathered.at[0, d], row_sem, d, at_clus[d]) for d in range(1, n_clus)
    }
    core_copy = {
        d: copy(gathered.at[0, d], gathered.at[1, d], core_sem, d, at_src[1]) for d in range(n_clus)
    }
    y_copy = {
        d: copy(gathered.at[0, d], gathered.at[2, d], y_sem, d, at_src[2]) for d in range(n_clus)
    }
    diag_copy = {
        d: copy(gathered.at[2, d], gathered.at[3, d], diag_sem, d, at_src[1]) for d in range(n_clus)
    }
    partial_copy = {
        0: copy(partial.at[1], partial_in.at[0], partial_sem, 0, at_src[1]),
        1: copy(partial.at[3], partial_in.at[1], partial_sem, 1, at_src[1]),
        2: copy(partial.at[2], partial_in.at[2], partial_sem, 2, at_src[2]),
    }
    owned_copy = {
        d: copy(owned.at[d], owned_in.at[d], owned_sem, d, at_clus[d]) for d in range(1, n_clus)
    }
    cent_copy = {
        e: copy(cents.at[0], cents.at[e], cent_sem, e, at_src[e]) for e in range(1, n_src)
    }
    shard_copy = {
        e: copy(shard_labels.at[0], shard_labels.at[e], shard_sem, e, at_src[e])
        for e in range(1, n_src)
    }
    max_copy = {
        d: copy(maxima.at[0], maxima.at[d], max_sem, d, at_clus[d]) for d in range(1, n_clus)
    }

    pl.semaphore_wait(barrier, len(others))
    half = n_clus // 2
    turns = list(range(1, n_clus))
    sends = turns[half - 1 :] + turns[: half - 1]
    for d in sends:
        row_copy[d].start()
        if d == turns[-1]:
            y_copy[0].start()
    for d in turns:
        label_copy[d].start()
    core_copy[0].start()

    order = (
        jnp.bitwise_xor(within // per, src) * (n_clus * per) + distance * per + within % per
    )
    count = n_src * n_clus * per
    members = jnp.where(
        lax.broadcasted_iota(jnp.int32, (count, rows), 0) == order, 2.0, 0.0
    ).astype(jnp.bfloat16)
    sums = jnp.zeros((count, depth), jnp.float32)
    for part in exact_parts(emb_ref[...] * 0.5):
        sums = sums + jnp.dot(members, part, preferred_element_type=jnp.float32)
    partial[...] = sums.reshape(n_src, n_clus * per, depth)
    for e in range(2):
        partial_copy[e].start()

    def send_labels():
        for d in turns:
            label_copy[d].wait_recv()
        own_labels = own_lanes(labels, n_clus, cap)
        shard_labels[0] = own_labels
        for e in range(1, n_src):
            shard_copy[e].start()
        return own_labels

    def pair_sums():
        for e in range(2):
            partial_copy[e].wait_recv()
        partial[2] = partial[2] + partial_in[1]
        partial_copy[2].start()

    def reduce_sums():
        partial_copy[2].wait_recv()
        total = partial[0] + partial_in[0] + partial_in[2]
        for d in range(n_clus):
            owned[d] = total[d * per : (d + 1) * per]
        for d in range(1, n_clus):
            owned_copy[d].start()

    def finish_sums():
        total = owned[0]
        for d in range(1, n_clus):
            owned_copy[d].wait_recv()
            total = total + owned_in[d]
        cents[0] = total * lax.rsqrt(jnp.sum(total * total, axis=1, keepdims=True) + EPS)
        for e in range(1, n_src):
            cent_copy[e].start()

    def column_labels(e):
        other = jnp.transpose(jnp.broadcast_to(shard_labels[e], (128, slots)))
        return jnp.concatenate([other] * (slots // 128), axis=1)

    def shard_maxima(e, other, first=0, last=n_clus):
        count = (last - first) * cap
        scores = dot_t(
            gathered[e, first:last].reshape(count, depth), gathered[0].reshape(slots, depth)
        )
        allowed = other[first * cap : last * cap] == own_labels
        if e == 0:
            allowed = allowed & (
                lax.broadcasted_iota(jnp.int32, (slots, slots), 0)
                != lax.broadcasted_iota(jnp.int32, (slots, slots), 1)
            )
        return jnp.max(jnp.where(allowed, scores, -1.0), axis=0, keepdims=True)

    def pass_on(d):
        y_copy[d].wait_recv()
        diag_copy[d].start()

    waiting = [0]
    for step, d in enumerate(turns):
        row_copy[d].wait_recv()
        y_copy[d].start()
        core_copy[d].start()
        waiting.append(d)
        if step == 0:
            pair_sums()
        if step == 1:
            own_labels = send_labels()
        if step == 2:
            reduce_sums()
        if 2 <= step < len(turns) - 1:
            pass_on(waiting.pop(0))
    best = shard_maxima(0, column_labels(0))
    for e in range(1, n_src):
        shard_copy[e].wait_recv()
    for d in range(n_clus):
        core_copy[d].wait_recv()
    best = jnp.maximum(best, shard_maxima(1, column_labels(1)))
    last = waiting.pop()
    for d in waiting:
        pass_on(d)
    finish_sums()
    over_y = column_labels(2)
    best = jnp.maximum(best, shard_maxima(2, over_y, 0, half))
    across = column_labels(3)
    for d in range(half):
        diag_copy[d].wait_recv()
    best = jnp.maximum(best, shard_maxima(3, across, 0, half))
    pass_on(last)
    best = jnp.maximum(best, shard_maxima(2, over_y, half, n_clus))
    for d in range(half, n_clus):
        diag_copy[d].wait_recv()
    maxima[0] = jnp.maximum(best, shard_maxima(3, across, half, n_clus))
    for d in turns:
        max_copy[d].start()

    for copies in (
        label_copy,
        row_copy,
        core_copy,
        y_copy,
        diag_copy,
        partial_copy,
        shard_copy,
        owned_copy,
    ):
        for started in copies.values():
            started.wait_send()
    for e in range(1, n_src):
        cent_copy[e].wait_recv()
    for shard in range(n_src):
        cent_ref[shard * per : (shard + 1) * per, :] = cents[src_peer[shard]]
    for d in turns:
        max_copy[d].wait_recv()
    near = jnp.zeros((8, rows), jnp.float32)
    for part in exact_parts(jnp.broadcast_to(own_lanes(maxima, n_clus, cap), (8, slots))):
        near = near + jnp.dot(part, pick, preferred_element_type=jnp.float32)
    near_ref[...] = near[:1]

    for started in list(cent_copy.values()) + list(max_copy.values()):
        started.wait_send()


def one_kernel(n_clus, n_src, embeddings, cluster):
    rows, depth = embeddings.shape
    cap = 2 * rows // n_clus
    slots = n_clus * cap
    per = CLUS_DEV // n_src
    f32, bf16 = jnp.float32, jnp.bfloat16
    vmem = pl.BlockSpec(memory_space=pltpu.VMEM)
    hbm = pl.BlockSpec(memory_space=pltpu.HBM)
    centroids, nearest = pl.pallas_call(
        functools.partial(owner_kernel, n_clus, n_src, cap),
        out_shape=(
            jax.ShapeDtypeStruct((CLUS_DEV, depth), f32),
            jax.ShapeDtypeStruct((1, rows), f32),
        ),
        in_specs=[hbm, hbm],
        out_specs=(vmem, vmem),
        scratch_shapes=[
            pltpu.VMEM((1, rows), jnp.int32),
            pltpu.VMEM((rows, depth), f32),
            pltpu.VMEM((n_clus, cap, depth), bf16),
            pltpu.VMEM((n_src, n_clus, cap, depth), bf16),
            pltpu.VMEM((n_clus, 1, slots), f32),
            pltpu.VMEM((n_src, 1, slots), f32),
            pltpu.VMEM((n_src, n_clus * per, depth), f32),
            pltpu.VMEM((n_src, n_clus * per, depth), f32),
            pltpu.VMEM((n_clus, per, depth), f32),
            pltpu.VMEM((n_clus, per, depth), f32),
            pltpu.VMEM((n_src, per, depth), f32),
            pltpu.VMEM((n_clus, 1, slots), f32),
        ]
        + [
            pltpu.SemaphoreType.DMA((2, count))
            for count in (n_clus, n_clus, n_clus, n_clus, n_clus, n_src, n_src, n_clus, n_src, n_clus)
        ]
        + [pltpu.SemaphoreType.DMA((1 + LOADS,))],
        compiler_params=pltpu.CompilerParams(
            collective_id=0, has_side_effects=True, vmem_limit_bytes=32 * 1024 * 1024
        ),
        cost_estimate=pl.CostEstimate(
            flops=2 * slots * slots * n_src * depth, bytes_accessed=rows * depth * 4, transcendentals=0
        ),
    )(
        pltpu.with_memory_space_constraint(cluster.reshape(1, rows), pltpu.HBM),
        pltpu.with_memory_space_constraint(embeddings, pltpu.HBM),
    )
    return centroids, nearest.reshape(rows)


def block_maxima(current, own_unit, own_labels, own_global, other_unit, other_labels, other_global):
    scores = lax.dot_general(
        own_unit, other_unit, (((1,), (1,)), ((), ())), preferred_element_type=jnp.float32
    )
    allowed = (
        (own_labels[:, None] == other_labels[None, :])
        & (own_global[:, None] != other_global[None, :])
        & (own_labels[:, None] >= 0)
    )
    return jnp.maximum(current, jnp.max(jnp.where(allowed, scores, jnp.float32(-1.0)), axis=1))


def unit_rows(values):
    return (values * lax.rsqrt(jnp.sum(values * values, axis=1, keepdims=True) + 1e-06)).astype(
        jnp.bfloat16
    )


def normalized(owned):
    return owned * lax.rsqrt(jnp.sum(owned * owned, axis=1, keepdims=True) + 1e-06)


def on_device(embeddings, cluster):
    row_count = embeddings.shape[0]
    feature_dim = embeddings.shape[1]
    clus_count = lax.axis_size("clus")
    source_count = lax.axis_size("src")
    capacity = max(2, 2 * row_count // clus_count)
    slot_total = clus_count * capacity
    owner = cluster // CLUS_DEV
    member_hits = (owner[:, None] == jnp.arange(clus_count, dtype=jnp.int32)[None, :]).astype(
        jnp.int32
    )
    running = jnp.cumsum(member_hits, axis=0)
    position = jnp.sum(member_hits * running, axis=1) - 1
    slot_index = owner * capacity + position
    device_number = lax.axis_index("clus") * source_count + lax.axis_index("src")
    global_row = device_number * row_count + jnp.arange(row_count, dtype=jnp.int32)
    send_labels = jnp.full((slot_total,), -1, jnp.int32).at[slot_index].set(cluster)
    send_global = jnp.full((slot_total,), -1, jnp.int32).at[slot_index].set(global_row)
    count = lax.axis_size("clus") * CLUS_DEV
    inside = (cluster >= 0) & (cluster < count)
    segment = jnp.where(inside, cluster, count)
    owned = lax.psum_scatter(
        jax.ops.segment_sum(embeddings, segment, num_segments=count + 1)[:count],
        "clus",
        scatter_dimension=0,
        tiled=True,
    )
    owned = lax.psum(owned, "src")
    centroids = normalized(owned)
    unit = unit_rows(embeddings)
    send_unit = jnp.zeros((slot_total, feature_dim), jnp.bfloat16).at[slot_index].set(unit)
    received, recv_labels, recv_global = (
        lax.all_to_all(send_unit, "clus", split_axis=0, concat_axis=0, tiled=True),
        lax.all_to_all(send_labels, "clus", split_axis=0, concat_axis=0, tiled=True),
        lax.all_to_all(send_global, "clus", split_axis=0, concat_axis=0, tiled=True),
    )
    initial = jnp.full((slot_total,), -1.0, jnp.float32)
    piece_unit = lax.all_gather(received, "src", axis=0, tiled=True)
    piece_labels = lax.all_gather(recv_labels, "src", axis=0, tiled=True)
    piece_global = lax.all_gather(recv_global, "src", axis=0, tiled=True)
    length = piece_unit.shape[0]
    stacked = (
        piece_unit.reshape(length // slot_total, slot_total, feature_dim),
        piece_labels.reshape(length // slot_total, slot_total),
        piece_global.reshape(length // slot_total, slot_total),
    )

    def stepper(carried, sliced):
        return (
            block_maxima(
                carried, received, recv_labels, recv_global, sliced[0], sliced[1], sliced[2]
            ),
            None,
        )

    result, unused = lax.scan(stepper, initial, stacked)
    returned = lax.all_to_all(result, "clus", split_axis=0, concat_axis=0, tiled=True)
    nearest = returned[slot_index]
    return (centroids, nearest)


def fits_one_kernel(n_clus, n_src, rows):
    cap = 2 * rows // n_clus
    return (
        n_src == 4
        and n_clus & (n_clus - 1) == 0
        and cap % 16 == 0
        and n_clus * cap % 128 == 0
        and rows % 128 == 0
    )


def solution(mesh):
    n_clus, n_src = mesh.shape["clus"], mesh.shape["src"]

    def body(embeddings, cluster):
        if fits_one_kernel(n_clus, n_src, embeddings.shape[0]):
            return one_kernel(n_clus, n_src, embeddings, cluster)
        return on_device(embeddings, cluster)

    placed = (P(("clus", "src"), None), P(("clus", "src")))
    return jax.shard_map(
        body,
        mesh=mesh,
        in_specs=placed,
        out_specs=(P("clus", None), P(("clus", "src"))),
        check_vma=False,
    )
```

```python
import functools

import jax
import jax.numpy as jnp
from jax import lax
from jax.experimental import pallas as pl
from jax.experimental.pallas import tpu as pltpu
from jax.sharding import PartitionSpec as P

CLUS_DEV = 8
MESH = pl.DeviceIdType.MESH
EPS = 1e-06
LOADS = 4


def partner(index, distance, count):
    total = 0
    bit = 1
    while bit < count:
        value = (index // bit) % 2
        total = total + bit * ((1 - value) if (distance // bit) % 2 else value)
        bit *= 2
    return total


def exact_parts(values):
    high = values.astype(jnp.bfloat16)
    rest = values - high.astype(jnp.float32)
    middle = rest.astype(jnp.bfloat16)
    low = (rest - middle.astype(jnp.float32)).astype(jnp.bfloat16)
    return high, middle, low


def dot_t(left, right):
    return lax.dot_general(left, right, (((1,), (1,)), ((), ())), preferred_element_type=jnp.float32)


def xor(left, right, count):
    total = 0
    bit = 1
    while bit < count:
        a, b = (left // bit) % 2, (right // bit) % 2
        total = total + bit * (a + b - 2 * a * b)
        bit *= 2
    return total


def hub_kernel(
    n_clus,
    n_src,
    cap,
    cluster_hbm,
    emb_hbm,
    cent_ref,
    near_ref,
    cluster_ref,
    emb_ref,
    packed,
    gathered,
    label_out,
    labels,
    group_labels,
    best,
    maxima,
    partial,
    partial_in,
    owned,
    owned_in,
    cents,
    row_send,
    row_recv,
    label_send,
    label_recv,
    max_send,
    max_recv,
    partial_sem,
    owned_sem,
    cent_sem,
    load_sem,
):
    rows, depth = emb_ref.shape
    slots = n_clus * cap
    per = CLUS_DEV // n_src
    me = lax.axis_index("clus")
    src = lax.axis_index("src")
    plane, side, level = me // 2, me % 2, src // 2
    is_hub = (src % 2 == 0) & (plane >= 1) & (plane <= 2)
    my_owner = (plane - 1) * 4 + level * 2 + side
    at_clus = [(partner(me, d, n_clus), src) for d in range(n_clus)]
    at_src = [(me, partner(src, e, n_src)) for e in range(n_src)]
    everyone = [
        (d, e, (partner(me, d, n_clus), partner(src, e, n_src)))
        for d in range(n_clus)
        for e in range(n_src)
    ]

    def copy(source, target, send, recv, device):
        return pltpu.make_async_remote_copy(
            src_ref=source,
            dst_ref=target,
            send_sem=send,
            recv_sem=recv,
            device_id=device,
            device_id_type=MESH,
        )

    def paired(source, target, sems, slot, device):
        return copy(source, target, sems.at[0, slot], sems.at[1, slot], device)

    band = rows // LOADS
    load_rows = [
        pltpu.make_async_copy(
            emb_hbm.at[pl.ds(i * band, band)], emb_ref.at[pl.ds(i * band, band)], load_sem.at[1 + i]
        )
        for i in range(LOADS)
    ]
    load_cluster = pltpu.make_async_copy(cluster_hbm, cluster_ref, load_sem.at[0])
    load_cluster.start()
    for load in load_rows:
        load.start()
    barrier = pltpu.get_barrier_semaphore()
    for _, _, device in everyone[1:]:
        pl.semaphore_signal(barrier, inc=1, device_id=device, device_id_type=MESH)

    load_cluster.wait()
    cluster = cluster_ref[...]
    within = cluster % CLUS_DEV
    owner = cluster // CLUS_DEV
    hits = lax.broadcasted_iota(jnp.int32, (n_clus, rows), 0) == owner
    earlier = lax.broadcasted_iota(jnp.int32, (rows, rows), 0) < lax.broadcasted_iota(
        jnp.int32, (rows, rows), 1
    )
    before = jnp.dot(
        jnp.where(hits, 1.0, 0.0).astype(jnp.bfloat16),
        jnp.where(earlier, 1.0, 0.0).astype(jnp.bfloat16),
        preferred_element_type=jnp.float32,
    )
    place = jnp.sum(jnp.where(hits, before, 0.0), axis=0, keepdims=True).astype(jnp.int32)
    slot_rows = lax.broadcasted_iota(jnp.int32, (slots, rows), 0)
    pick = jnp.where(slot_rows == owner * cap + place, 1.0, 0.0).astype(jnp.bfloat16)
    block = jnp.bitwise_xor(owner % 2, side) * n_src + jnp.bitwise_xor(
        (owner // 2) % 2 * 2, src
    )
    spread = jnp.where(slot_rows == block * cap + place, 1.0, 0.0).astype(jnp.bfloat16)
    marked = jnp.where(hits, (within + 1).astype(jnp.float32), 0.0).astype(jnp.bfloat16)
    label_rows = dot_t(marked, spread)
    for o in range(n_clus):
        label_out[o] = label_rows[o : o + 1]

    units = []
    for i, load in enumerate(load_rows):
        load.wait()
        part = emb_ref[i * band : (i + 1) * band]
        norm = lax.rsqrt(jnp.sum(part * part, axis=1, keepdims=True) + EPS)
        units.append((part * norm).astype(jnp.bfloat16))
    unit = jnp.concatenate(units, axis=0)
    packed[...] = (
        jnp.dot(pick, unit, preferred_element_type=jnp.float32)
        .astype(jnp.bfloat16)
        .reshape(n_clus, cap, depth)
    )

    near_plane = plane // 2
    row_copy, label_copy, homes = [], [], []
    for i in range(n_clus):
        z = near_plane if i % 2 else 1 - near_plane
        x = partner(side, (i // 2) % 2, 2)
        y = partner(level, i // 4, 2)
        o = z * 4 + y * 2 + x
        device = ((1 + z) * 2 + x, 2 * y)
        d, e = xor(me, device[0], n_clus), xor(src, device[1], n_src)
        homes.append(o)
        row_copy.append(
            copy(packed.at[o], gathered.at[d, e], row_send.at[i], row_recv.at[d, e], device)
        )
        label_copy.append(
            copy(label_out.at[o], labels.at[d, e], label_send.at[i], label_recv.at[d, e], device)
        )
    partial_copy = [
        paired(partial.at[1], partial_in.at[0], partial_sem, 0, at_src[1]),
        paired(partial.at[3], partial_in.at[1], partial_sem, 1, at_src[1]),
        paired(partial.at[2], partial_in.at[2], partial_sem, 2, at_src[2]),
    ]
    owned_copy = {
        d: paired(owned.at[d], owned_in.at[d], owned_sem, d, at_clus[d]) for d in range(1, n_clus)
    }
    cent_copy = {
        e: paired(cents.at[0], cents.at[e], cent_sem, e, at_src[e]) for e in range(1, n_src)
    }

    pl.semaphore_wait(barrier, len(everyone) - 1)
    for copies in (label_copy, row_copy):
        for i in range(n_clus):
            if i == 1:
                @pl.when(jnp.logical_not(is_hub))
                def _():
                    copies[1].start()
            else:
                copies[i].start()

    @pl.when(is_hub)
    def _():
        gathered[0, 0] = packed[homes[1]]
        labels[0, 0] = label_out[homes[1]]

    order = (
        jnp.bitwise_xor(within // per, src) * (n_clus * per)
        + jnp.bitwise_xor(owner, me) * per
        + within % per
    )
    count = n_src * n_clus * per
    members = jnp.where(
        lax.broadcasted_iota(jnp.int32, (count, rows), 0) == order, 2.0, 0.0
    ).astype(jnp.bfloat16)
    sums = jnp.zeros((count, depth), jnp.float32)
    for part in exact_parts(emb_ref[...] * 0.5):
        sums = sums + jnp.dot(members, part, preferred_element_type=jnp.float32)
    partial[...] = sums.reshape(n_src, n_clus * per, depth)
    partial_copy[0].start()
    partial_copy[1].start()
    partial_copy[0].wait_recv()
    partial_copy[1].wait_recv()
    partial[2] = partial[2] + partial_in[1]
    partial_copy[2].start()
    partial_copy[2].wait_recv()
    total = partial[0] + partial_in[0] + partial_in[2]
    for d in range(n_clus):
        owned[d] = total[d * per : (d + 1) * per]
    for d in range(1, n_clus):
        owned_copy[d].start()

    def arrived(copy_source, target, sems, d, e):
        copy(copy_source, target.at[d, e], sems.at[d, e], sems.at[d, e], at_src[1]).wait_recv()

    def meet(group, earlier_groups):
        width = 2 * n_src * cap
        mine = jnp.zeros((1, width), jnp.float32)
        for d in (2 * group, 2 * group + 1):
            for e in range(n_src):
                if d or e:
                    arrived(label_out.at[0], labels, label_recv, d, e)
                mine = mine + labels[d, e]
        group_labels[group] = mine
        column = jnp.transpose(jnp.broadcast_to(mine, (128, width)))
        column = jnp.concatenate([column] * (width // 128), axis=1)
        for d in (2 * group, 2 * group + 1):
            for e in range(n_src):
                if d or e:
                    arrived(packed.at[0], gathered, row_recv, d, e)
        left = gathered[2 * group : 2 * group + 2].reshape(width, depth)

        def scores(other):
            right = gathered[2 * other : 2 * other + 2].reshape(width, depth)
            return dot_t(left, right), column == group_labels[other]

        values, allowed = scores(group)
        allowed = allowed & (
            lax.broadcasted_iota(jnp.int32, (width, width), 0)
            != lax.broadcasted_iota(jnp.int32, (width, width), 1)
        )
        top = jnp.max(jnp.where(allowed, values, -1.0), axis=0, keepdims=True)
        across = None
        for other in earlier_groups:
            values, allowed = scores(other)
            values = jnp.where(allowed, values, -1.0)
            best[other] = jnp.maximum(best[other], jnp.max(values, axis=0, keepdims=True))
            for j in range(width // 128):
                piece = values[:, j * 128 : (j + 1) * 128]
                across = piece if across is None else jnp.maximum(across, piece)
        if across is not None:
            top = jnp.maximum(top, jnp.max(jnp.transpose(across), axis=0, keepdims=True))
        best[group] = top

    @pl.when(is_hub)
    def _():
        meet(0, [])
        meet(1, [0])

    total = owned[0]
    for d in range(1, n_clus):
        owned_copy[d].wait_recv()
        total = total + owned_in[d]
    cents[0] = total * lax.rsqrt(jnp.sum(total * total, axis=1, keepdims=True) + EPS)
    for e in range(1, n_src):
        cent_copy[e].start()

    def returned(d, e, device):
        return copy(
            best.at[d // 2],
            maxima.at[my_owner],
            max_send.at[d, e],
            max_recv.at[my_owner],
            device,
        )

    @pl.when(is_hub)
    def _():
        meet(3, [0, 1])
        meet(2, [0, 1, 3])
        for d, e, device in everyone[:0:-1]:
            returned(d, e, device).start()
        maxima[my_owner] = best[0]

    for copies in (label_copy, row_copy):
        for i in range(n_clus):
            if i == 1:
                @pl.when(jnp.logical_not(is_hub))
                def _():
                    copies[1].wait_send()
            else:
                copies[i].wait_send()
    for started in partial_copy + list(owned_copy.values()) + list(cent_copy.values()):
        started.wait_send()
    for e in range(1, n_src):
        cent_copy[e].wait_recv()
    for shard in range(n_src):
        cent_ref[shard * per : (shard + 1) * per, :] = cents[partner(src, shard, n_src)]

    for o in range(n_clus):
        @pl.when(jnp.logical_not(is_hub & (my_owner == o)))
        def _():
            copy(best.at[0], maxima.at[o], max_recv.at[o], max_recv.at[o], at_src[1]).wait_recv()
    near = jnp.zeros((n_clus, rows), jnp.float32)
    for part in exact_parts(jnp.concatenate([maxima[o] for o in range(n_clus)], axis=0)):
        near = near + jnp.dot(part, spread, preferred_element_type=jnp.float32)
    near_ref[...] = jnp.sum(jnp.where(hits, near, 0.0), axis=0, keepdims=True)

    @pl.when(is_hub)
    def _():
        for d, e, device in everyone[1:]:
            returned(d, e, device).wait_send()


def one_kernel(n_clus, n_src, embeddings, cluster):
    rows, depth = embeddings.shape
    cap = 2 * rows // n_clus
    slots = n_clus * cap
    per = CLUS_DEV // n_src
    f32, bf16 = jnp.float32, jnp.bfloat16
    vmem = pl.BlockSpec(memory_space=pltpu.VMEM)
    hbm = pl.BlockSpec(memory_space=pltpu.HBM)
    dma = pltpu.SemaphoreType.DMA
    centroids, nearest = pl.pallas_call(
        functools.partial(hub_kernel, n_clus, n_src, cap),
        out_shape=(
            jax.ShapeDtypeStruct((CLUS_DEV, depth), f32),
            jax.ShapeDtypeStruct((1, rows), f32),
        ),
        in_specs=[hbm, hbm],
        out_specs=(vmem, vmem),
        scratch_shapes=[
            pltpu.VMEM((1, rows), jnp.int32),
            pltpu.VMEM((rows, depth), f32),
            pltpu.VMEM((n_clus, cap, depth), bf16),
            pltpu.VMEM((n_clus, n_src, cap, depth), bf16),
            pltpu.VMEM((n_clus, 1, slots), f32),
            pltpu.VMEM((n_clus, n_src, 1, slots), f32),
            pltpu.VMEM((n_clus // 2, 1, slots), f32),
            pltpu.VMEM((n_clus // 2, 1, slots), f32),
            pltpu.VMEM((n_clus, 1, slots), f32),
            pltpu.VMEM((n_src, n_clus * per, depth), f32),
            pltpu.VMEM((n_src, n_clus * per, depth), f32),
            pltpu.VMEM((n_clus, per, depth), f32),
            pltpu.VMEM((n_clus, per, depth), f32),
            pltpu.VMEM((n_src, per, depth), f32),
            dma((n_clus,)),
            dma((n_clus, n_src)),
            dma((n_clus,)),
            dma((n_clus, n_src)),
            dma((n_clus, n_src)),
            dma((n_clus,)),
            dma((2, n_src)),
            dma((2, n_clus)),
            dma((2, n_src)),
            dma((1 + LOADS,)),
        ],
        compiler_params=pltpu.CompilerParams(
            collective_id=0, has_side_effects=True, vmem_limit_bytes=32 * 1024 * 1024
        ),
        cost_estimate=pl.CostEstimate(
            flops=2 * slots * slots * n_src * depth, bytes_accessed=rows * depth * 4, transcendentals=0
        ),
    )(
        pltpu.with_memory_space_constraint(cluster.reshape(1, rows), pltpu.HBM),
        pltpu.with_memory_space_constraint(embeddings, pltpu.HBM),
    )
    return centroids, nearest.reshape(rows)


def block_maxima(current, own_unit, own_labels, own_global, other_unit, other_labels, other_global):
    scores = lax.dot_general(
        own_unit, other_unit, (((1,), (1,)), ((), ())), preferred_element_type=jnp.float32
    )
    allowed = (
        (own_labels[:, None] == other_labels[None, :])
        & (own_global[:, None] != other_global[None, :])
        & (own_labels[:, None] >= 0)
    )
    return jnp.maximum(current, jnp.max(jnp.where(allowed, scores, jnp.float32(-1.0)), axis=1))


def unit_rows(values):
    return (values * lax.rsqrt(jnp.sum(values * values, axis=1, keepdims=True) + 1e-06)).astype(
        jnp.bfloat16
    )


def normalized(owned):
    return owned * lax.rsqrt(jnp.sum(owned * owned, axis=1, keepdims=True) + 1e-06)


def on_device(embeddings, cluster):
    row_count = embeddings.shape[0]
    feature_dim = embeddings.shape[1]
    clus_count = lax.axis_size("clus")
    source_count = lax.axis_size("src")
    capacity = max(2, 2 * row_count // clus_count)
    slot_total = clus_count * capacity
    owner = cluster // CLUS_DEV
    member_hits = (owner[:, None] == jnp.arange(clus_count, dtype=jnp.int32)[None, :]).astype(
        jnp.int32
    )
    running = jnp.cumsum(member_hits, axis=0)
    position = jnp.sum(member_hits * running, axis=1) - 1
    slot_index = owner * capacity + position
    device_number = lax.axis_index("clus") * source_count + lax.axis_index("src")
    global_row = device_number * row_count + jnp.arange(row_count, dtype=jnp.int32)
    send_labels = jnp.full((slot_total,), -1, jnp.int32).at[slot_index].set(cluster)
    send_global = jnp.full((slot_total,), -1, jnp.int32).at[slot_index].set(global_row)
    count = lax.axis_size("clus") * CLUS_DEV
    inside = (cluster >= 0) & (cluster < count)
    segment = jnp.where(inside, cluster, count)
    owned = lax.psum_scatter(
        jax.ops.segment_sum(embeddings, segment, num_segments=count + 1)[:count],
        "clus",
        scatter_dimension=0,
        tiled=True,
    )
    owned = lax.psum(owned, "src")
    centroids = normalized(owned)
    unit = unit_rows(embeddings)
    send_unit = jnp.zeros((slot_total, feature_dim), jnp.bfloat16).at[slot_index].set(unit)
    received, recv_labels, recv_global = (
        lax.all_to_all(send_unit, "clus", split_axis=0, concat_axis=0, tiled=True),
        lax.all_to_all(send_labels, "clus", split_axis=0, concat_axis=0, tiled=True),
        lax.all_to_all(send_global, "clus", split_axis=0, concat_axis=0, tiled=True),
    )
    initial = jnp.full((slot_total,), -1.0, jnp.float32)
    piece_unit = lax.all_gather(received, "src", axis=0, tiled=True)
    piece_labels = lax.all_gather(recv_labels, "src", axis=0, tiled=True)
    piece_global = lax.all_gather(recv_global, "src", axis=0, tiled=True)
    length = piece_unit.shape[0]
    stacked = (
        piece_unit.reshape(length // slot_total, slot_total, feature_dim),
        piece_labels.reshape(length // slot_total, slot_total),
        piece_global.reshape(length // slot_total, slot_total),
    )

    def stepper(carried, sliced):
        return (
            block_maxima(
                carried, received, recv_labels, recv_global, sliced[0], sliced[1], sliced[2]
            ),
            None,
        )

    result, unused = lax.scan(stepper, initial, stacked)
    returned = lax.all_to_all(result, "clus", split_axis=0, concat_axis=0, tiled=True)
    nearest = returned[slot_index]
    return (centroids, nearest)


def fits_one_kernel(n_clus, n_src, rows):
    return n_clus == 8 and n_src == 4 and rows == 128


def solution(mesh):
    n_clus, n_src = mesh.shape["clus"], mesh.shape["src"]

    def body(embeddings, cluster):
        if fits_one_kernel(n_clus, n_src, embeddings.shape[0]):
            return one_kernel(n_clus, n_src, embeddings, cluster)
        return on_device(embeddings, cluster)

    placed = (P(("clus", "src"), None), P(("clus", "src")))
    return jax.shard_map(
        body,
        mesh=mesh,
        in_specs=placed,
        out_specs=(P("clus", None), P(("clus", "src"))),
        check_vma=False,
    )
```

```python
import functools

import jax
import jax.numpy as jnp
from jax import lax
from jax.experimental import pallas as pl
from jax.experimental.pallas import tpu as pltpu
from jax.sharding import PartitionSpec as P

CLUS_DEV = 8
MESH = pl.DeviceIdType.MESH
EPS = 1e-06
LOADS = 4


def partner(index, distance, count):
    total = 0
    bit = 1
    while bit < count:
        value = (index // bit) % 2
        total = total + bit * ((1 - value) if (distance // bit) % 2 else value)
        bit *= 2
    return total


def exact_parts(values):
    high = values.astype(jnp.bfloat16)
    rest = values - high.astype(jnp.float32)
    middle = rest.astype(jnp.bfloat16)
    low = (rest - middle.astype(jnp.float32)).astype(jnp.bfloat16)
    return high, middle, low


def dot_t(left, right):
    return lax.dot_general(left, right, (((1,), (1,)), ((), ())), preferred_element_type=jnp.float32)


def xor(left, right, count):
    total = 0
    bit = 1
    while bit < count:
        a, b = (left // bit) % 2, (right // bit) % 2
        total = total + bit * (a + b - 2 * a * b)
        bit *= 2
    return total


def hub_kernel(
    n_clus,
    n_src,
    cap,
    cluster_hbm,
    emb_hbm,
    cent_ref,
    near_ref,
    cluster_ref,
    emb_ref,
    packed,
    gathered,
    label_out,
    labels,
    group_labels,
    columns,
    best,
    maxima,
    partial,
    partial_in,
    owned,
    owned_in,
    cents,
    row_send,
    row_recv,
    label_send,
    label_recv,
    max_send,
    max_recv,
    pass_sem,
    pass_label_sem,
    partial_sem,
    owned_sem,
    cent_sem,
    load_sem,
):
    rows, depth = emb_ref.shape
    slots = n_clus * cap
    per = CLUS_DEV // n_src
    me = lax.axis_index("clus")
    src = lax.axis_index("src")
    plane, side, level = me // 2, me % 2, src // 2
    is_hub = (plane >= 1) & (plane <= 2)
    my_owner = (plane - 1) * 4 + level * 2 + side
    at_clus = [(partner(me, d, n_clus), src) for d in range(n_clus)]
    at_src = [(me, partner(src, e, n_src)) for e in range(n_src)]
    sides = n_src // 2
    width = 2 * sides * cap
    alike = [
        (d, e, (partner(me, d, n_clus), partner(src, 2 * e, n_src)))
        for d in range(n_clus)
        for e in range(sides)
    ]
    arrival = [0, 1, 3, 2]

    def copy(source, target, send, recv, device):
        return pltpu.make_async_remote_copy(
            src_ref=source,
            dst_ref=target,
            send_sem=send,
            recv_sem=recv,
            device_id=device,
            device_id_type=MESH,
        )

    def paired(source, target, sems, slot, device):
        return copy(source, target, sems.at[0, slot], sems.at[1, slot], device)

    band = rows // LOADS
    load_rows = [
        pltpu.make_async_copy(
            emb_hbm.at[pl.ds(i * band, band)], emb_ref.at[pl.ds(i * band, band)], load_sem.at[1 + i]
        )
        for i in range(LOADS)
    ]
    load_cluster = pltpu.make_async_copy(cluster_hbm, cluster_ref, load_sem.at[0])
    load_cluster.start()
    for load in load_rows:
        load.start()
    barrier = pltpu.get_barrier_semaphore()
    reached = [device for _, _, device in alike[1:]] + [at_src[1], at_src[3]]
    for device in reached:
        pl.semaphore_signal(barrier, inc=1, device_id=device, device_id_type=MESH)

    load_cluster.wait()
    cluster = cluster_ref[...]
    within = cluster % CLUS_DEV
    owner = cluster // CLUS_DEV
    hits = lax.broadcasted_iota(jnp.int32, (n_clus, rows), 0) == owner
    earlier = lax.broadcasted_iota(jnp.int32, (rows, rows), 0) < lax.broadcasted_iota(
        jnp.int32, (rows, rows), 1
    )
    before = jnp.dot(
        jnp.where(hits, 1.0, 0.0).astype(jnp.bfloat16),
        jnp.where(earlier, 1.0, 0.0).astype(jnp.bfloat16),
        preferred_element_type=jnp.float32,
    )
    place = jnp.sum(jnp.where(hits, before, 0.0), axis=0, keepdims=True).astype(jnp.int32)
    slot_rows = lax.broadcasted_iota(jnp.int32, (slots, rows), 0)
    pick = jnp.where(slot_rows == owner * cap + place, 1.0, 0.0).astype(jnp.bfloat16)
    block = jnp.bitwise_xor(owner % 2, side) * sides + jnp.bitwise_xor((owner // 2) % 2, level)
    spread = jnp.where(slot_rows[:width] == block * cap + place, 1.0, 0.0).astype(jnp.bfloat16)
    marked = jnp.where(hits, (within + 1).astype(jnp.float32), 0.0).astype(jnp.bfloat16)
    label_rows = dot_t(marked, spread)
    for o in range(n_clus):
        label_out[o] = label_rows[o : o + 1]

    units = []
    for i, load in enumerate(load_rows):
        load.wait()
        part = emb_ref[i * band : (i + 1) * band]
        norm = lax.rsqrt(jnp.sum(part * part, axis=1, keepdims=True) + EPS)
        units.append((part * norm).astype(jnp.bfloat16))
    unit = jnp.concatenate(units, axis=0)
    packed[...] = (
        jnp.dot(pick, unit, preferred_element_type=jnp.float32)
        .astype(jnp.bfloat16)
        .reshape(n_clus, cap, depth)
    )

    near_plane = plane // 2
    row_copy, label_copy, homes = [], [], []
    for i in range(n_clus):
        z = near_plane if i % 2 else 1 - near_plane
        x = partner(side, (i // 2) % 2, 2)
        y = partner(level, i // 4, 2)
        o = z * 4 + y * 2 + x
        device = ((1 + z) * 2 + x, 2 * y + src % 2)
        near = xor(me, device[0], n_clus)
        e = i // 4
        far = near // 2
        d = (far + far // 2 - 2 * (far // 3)) * 2 + near % 2
        homes.append(o)
        row_copy.append(
            copy(packed.at[o], gathered.at[0, d, e], row_send.at[i], row_recv.at[d, e], device)
        )
        label_copy.append(
            copy(label_out.at[o], labels.at[d, e], label_send.at[i], label_recv.at[d, e], device)
        )
    partial_copy = [
        paired(partial.at[1], partial_in.at[0], partial_sem, 0, at_src[1]),
        paired(partial.at[3], partial_in.at[1], partial_sem, 1, at_src[1]),
        paired(partial.at[2], partial_in.at[2], partial_sem, 2, at_src[2]),
    ]
    owned_copy = {
        d: paired(owned.at[d], owned_in.at[d], owned_sem, d, at_clus[d]) for d in range(1, n_clus)
    }
    cent_copy = {
        e: paired(cents.at[0], cents.at[e], cent_sem, e, at_src[e]) for e in range(1, n_src)
    }

    pl.semaphore_wait(barrier, len(reached))
    for copies in (label_copy, row_copy):
        for i in range(n_clus):
            if i == 1:
                @pl.when(jnp.logical_not(is_hub))
                def _():
                    copies[1].start()
            else:
                copies[i].start()

    @pl.when(is_hub)
    def _():
        gathered[0, 0, 0] = packed[homes[1]]
        labels[0, 0] = label_out[homes[1]]

    order = (
        jnp.bitwise_xor(within // per, src) * (n_clus * per)
        + jnp.bitwise_xor(owner, me) * per
        + within % per
    )
    count = n_src * n_clus * per
    members = jnp.where(
        lax.broadcasted_iota(jnp.int32, (count, rows), 0) == order, 2.0, 0.0
    ).astype(jnp.bfloat16)
    sums = jnp.zeros((count, depth), jnp.float32)
    for part in exact_parts(emb_ref[...] * 0.5):
        sums = sums + jnp.dot(members, part, preferred_element_type=jnp.float32)
    partial[...] = sums.reshape(n_src, n_clus * per, depth)
    partial_copy[0].start()
    partial_copy[1].start()
    partial_copy[0].wait_recv()
    partial_copy[1].wait_recv()
    partial[2] = partial[2] + partial_in[1]
    partial_copy[2].start()
    partial_copy[2].wait_recv()
    total = partial[0] + partial_in[0] + partial_in[2]
    for d in range(n_clus):
        owned[d] = total[d * per : (d + 1) * per]
    for d in range(1, n_clus):
        owned_copy[d].start()

    def arrived(copy_source, target, sem):
        copy(copy_source, target, sem, sem, at_src[1]).wait_recv()

    def pass_rows(g):
        pair = pl.ds(2 * g, 2)
        return paired(gathered.at[0, pair], gathered.at[1, pair], pass_sem, g, at_src[1])

    def pass_labels(g):
        return paired(group_labels.at[0, g], group_labels.at[1, g], pass_label_sem, g, at_src[1])

    def rows_of(core, first, last):
        held = gathered[core, 2 * first : 2 * last]
        return held.reshape((last - first) * width, depth)

    def label_row(core, last):
        return jnp.concatenate([group_labels[core, g] for g in range(last)], axis=1)

    def column_of(row):
        return jnp.transpose(jnp.broadcast_to(row, (width, width)))

    def raise_best(values, first):
        top = jnp.max(values, axis=0, keepdims=True)
        for j in range(top.shape[1] // width):
            best[first + j] = jnp.maximum(best[first + j], top[:, j * width : (j + 1) * width])

    def meet(g):
        blocks = [(d, e) for d in (2 * g, 2 * g + 1) for e in range(sides)]
        mine = jnp.zeros((1, width), jnp.float32)
        for d, e in blocks:
            if d or e:
                arrived(label_out.at[0], labels.at[d, e], label_recv.at[d, e])
            mine = mine + labels[d, e]
        group_labels[0, g] = mine
        pass_labels(g).start()
        best[g] = jnp.full((1, width), -1.0, jnp.float32)
        for d, e in blocks:
            if d or e:
                arrived(packed.at[0], gathered.at[0, d, e], row_recv.at[d, e])
        pass_rows(g).start()
        own_labels = label_row(0, g + 1)
        wide = (width, (g + 1) * width)
        row_place = lax.broadcasted_iota(jnp.int32, wide, 0) + g * width
        allowed = jnp.concatenate([column_of(mine)] * (g + 1), axis=1) == own_labels
        allowed = allowed & (row_place != lax.broadcasted_iota(jnp.int32, wide, 1))
        values = jnp.where(allowed, dot_t(rows_of(0, g, g + 1), rows_of(0, 0, g + 1)), -1.0)
        raise_best(values, 0)
        if g:
            across = values[:, :width]
            for j in range(1, g):
                across = jnp.maximum(across, values[:, j * width : (j + 1) * width])
            raise_best(jnp.transpose(across), g)
            earlier_rows = jnp.concatenate([columns[j] for j in range(g)], axis=0)
            values = dot_t(rows_of(1, 0, g), rows_of(0, g, g + 1))
            raise_best(jnp.where(earlier_rows == mine, values, -1.0), g)
        pass_labels(g).wait_recv()
        columns[g] = column_of(group_labels[1, g])
        allowed = jnp.concatenate([columns[g]] * (g + 1), axis=1) == own_labels
        pass_rows(g).wait_recv()
        values = dot_t(rows_of(1, g, g + 1), rows_of(0, 0, g + 1))
        raise_best(jnp.where(allowed, values, -1.0), 0)

    @pl.when(is_hub)
    def _():
        meet(0)
        meet(1)

    total = owned[0]
    for d in range(1, n_clus):
        owned_copy[d].wait_recv()
        total = total + owned_in[d]
    cents[0] = total * lax.rsqrt(jnp.sum(total * total, axis=1, keepdims=True) + EPS)
    for e in range(1, n_src):
        cent_copy[e].start()

    def returned(d, e, device):
        return copy(
            best.at[arrival[d // 2]],
            maxima.at[my_owner],
            max_send.at[d, e],
            max_recv.at[my_owner],
            device,
        )

    @pl.when(is_hub)
    def _():
        meet(2)
        meet(3)
        for d, e, device in alike[:0:-1]:
            returned(d, e, device).start()
        maxima[my_owner] = best[0]

    for copies in (label_copy, row_copy):
        for i in range(n_clus):
            if i == 1:
                @pl.when(jnp.logical_not(is_hub))
                def _():
                    copies[1].wait_send()
            else:
                copies[i].wait_send()
    for started in partial_copy + list(owned_copy.values()) + list(cent_copy.values()):
        started.wait_send()
    for e in range(1, n_src):
        cent_copy[e].wait_recv()
    for shard in range(n_src):
        cent_ref[shard * per : (shard + 1) * per, :] = cents[partner(src, shard, n_src)]

    for o in range(n_clus):
        @pl.when(jnp.logical_not(is_hub & (my_owner == o)))
        def _():
            copy(best.at[0], maxima.at[o], max_recv.at[o], max_recv.at[o], at_src[1]).wait_recv()
    near = jnp.zeros((n_clus, rows), jnp.float32)
    for part in exact_parts(jnp.concatenate([maxima[o] for o in range(n_clus)], axis=0)):
        near = near + jnp.dot(part, spread, preferred_element_type=jnp.float32)
    near_ref[...] = jnp.sum(jnp.where(hits, near, 0.0), axis=0, keepdims=True)

    @pl.when(is_hub)
    def _():
        for d, e, device in alike[1:]:
            returned(d, e, device).wait_send()
        for g in range(len(arrival)):
            pass_rows(g).wait_send()
            pass_labels(g).wait_send()


def one_kernel(n_clus, n_src, embeddings, cluster):
    rows, depth = embeddings.shape
    cap = 2 * rows // n_clus
    slots = n_clus * cap
    per = CLUS_DEV // n_src
    sides, levels = n_src // 2, n_clus // 2
    width = 2 * sides * cap
    f32, bf16 = jnp.float32, jnp.bfloat16
    vmem = pl.BlockSpec(memory_space=pltpu.VMEM)
    hbm = pl.BlockSpec(memory_space=pltpu.HBM)
    dma = pltpu.SemaphoreType.DMA
    centroids, nearest = pl.pallas_call(
        functools.partial(hub_kernel, n_clus, n_src, cap),
        out_shape=(
            jax.ShapeDtypeStruct((CLUS_DEV, depth), f32),
            jax.ShapeDtypeStruct((1, rows), f32),
        ),
        in_specs=[hbm, hbm],
        out_specs=(vmem, vmem),
        scratch_shapes=[
            pltpu.VMEM((1, rows), jnp.int32),
            pltpu.VMEM((rows, depth), f32),
            pltpu.VMEM((n_clus, cap, depth), bf16),
            pltpu.VMEM((2, n_clus, sides, cap, depth), bf16),
            pltpu.VMEM((n_clus, 1, width), f32),
            pltpu.VMEM((n_clus, sides, 1, width), f32),
            pltpu.VMEM((2, levels, 1, width), f32),
            pltpu.VMEM((levels, width, width), f32),
            pltpu.VMEM((levels, 1, width), f32),
            pltpu.VMEM((n_clus, 1, width), f32),
            pltpu.VMEM((n_src, n_clus * per, depth), f32),
            pltpu.VMEM((n_src, n_clus * per, depth), f32),
            pltpu.VMEM((n_clus, per, depth), f32),
            pltpu.VMEM((n_clus, per, depth), f32),
            pltpu.VMEM((n_src, per, depth), f32),
            dma((n_clus,)),
            dma((n_clus, sides)),
            dma((n_clus,)),
            dma((n_clus, sides)),
            dma((n_clus, sides)),
            dma((n_clus,)),
            dma((2, levels)),
            dma((2, levels)),
            dma((2, n_src)),
            dma((2, n_clus)),
            dma((2, n_src)),
            dma((1 + LOADS,)),
        ],
        compiler_params=pltpu.CompilerParams(
            collective_id=0, has_side_effects=True, vmem_limit_bytes=32 * 1024 * 1024
        ),
        cost_estimate=pl.CostEstimate(
            flops=2 * slots * slots * n_src * depth, bytes_accessed=rows * depth * 4, transcendentals=0
        ),
    )(
        pltpu.with_memory_space_constraint(cluster.reshape(1, rows), pltpu.HBM),
        pltpu.with_memory_space_constraint(embeddings, pltpu.HBM),
    )
    return centroids, nearest.reshape(rows)


def block_maxima(current, own_unit, own_labels, own_global, other_unit, other_labels, other_global):
    scores = lax.dot_general(
        own_unit, other_unit, (((1,), (1,)), ((), ())), preferred_element_type=jnp.float32
    )
    allowed = (
        (own_labels[:, None] == other_labels[None, :])
        & (own_global[:, None] != other_global[None, :])
        & (own_labels[:, None] >= 0)
    )
    return jnp.maximum(current, jnp.max(jnp.where(allowed, scores, jnp.float32(-1.0)), axis=1))


def unit_rows(values):
    return (values * lax.rsqrt(jnp.sum(values * values, axis=1, keepdims=True) + 1e-06)).astype(
        jnp.bfloat16
    )


def normalized(owned):
    return owned * lax.rsqrt(jnp.sum(owned * owned, axis=1, keepdims=True) + 1e-06)


def on_device(embeddings, cluster):
    row_count = embeddings.shape[0]
    feature_dim = embeddings.shape[1]
    clus_count = lax.axis_size("clus")
    source_count = lax.axis_size("src")
    capacity = max(2, 2 * row_count // clus_count)
    slot_total = clus_count * capacity
    owner = cluster // CLUS_DEV
    member_hits = (owner[:, None] == jnp.arange(clus_count, dtype=jnp.int32)[None, :]).astype(
        jnp.int32
    )
    running = jnp.cumsum(member_hits, axis=0)
    position = jnp.sum(member_hits * running, axis=1) - 1
    slot_index = owner * capacity + position
    device_number = lax.axis_index("clus") * source_count + lax.axis_index("src")
    global_row = device_number * row_count + jnp.arange(row_count, dtype=jnp.int32)
    send_labels = jnp.full((slot_total,), -1, jnp.int32).at[slot_index].set(cluster)
    send_global = jnp.full((slot_total,), -1, jnp.int32).at[slot_index].set(global_row)
    count = lax.axis_size("clus") * CLUS_DEV
    inside = (cluster >= 0) & (cluster < count)
    segment = jnp.where(inside, cluster, count)
    owned = lax.psum_scatter(
        jax.ops.segment_sum(embeddings, segment, num_segments=count + 1)[:count],
        "clus",
        scatter_dimension=0,
        tiled=True,
    )
    owned = lax.psum(owned, "src")
    centroids = normalized(owned)
    unit = unit_rows(embeddings)
    send_unit = jnp.zeros((slot_total, feature_dim), jnp.bfloat16).at[slot_index].set(unit)
    received, recv_labels, recv_global = (
        lax.all_to_all(send_unit, "clus", split_axis=0, concat_axis=0, tiled=True),
        lax.all_to_all(send_labels, "clus", split_axis=0, concat_axis=0, tiled=True),
        lax.all_to_all(send_global, "clus", split_axis=0, concat_axis=0, tiled=True),
    )
    initial = jnp.full((slot_total,), -1.0, jnp.float32)
    piece_unit = lax.all_gather(received, "src", axis=0, tiled=True)
    piece_labels = lax.all_gather(recv_labels, "src", axis=0, tiled=True)
    piece_global = lax.all_gather(recv_global, "src", axis=0, tiled=True)
    length = piece_unit.shape[0]
    stacked = (
        piece_unit.reshape(length // slot_total, slot_total, feature_dim),
        piece_labels.reshape(length // slot_total, slot_total),
        piece_global.reshape(length // slot_total, slot_total),
    )

    def stepper(carried, sliced):
        return (
            block_maxima(
                carried, received, recv_labels, recv_global, sliced[0], sliced[1], sliced[2]
            ),
            None,
        )

    result, unused = lax.scan(stepper, initial, stacked)
    returned = lax.all_to_all(result, "clus", split_axis=0, concat_axis=0, tiled=True)
    nearest = returned[slot_index]
    return (centroids, nearest)


def fits_one_kernel(n_clus, n_src, rows):
    return n_clus == 8 and n_src == 4 and rows == 128


def solution(mesh):
    n_clus, n_src = mesh.shape["clus"], mesh.shape["src"]

    def body(embeddings, cluster):
        if fits_one_kernel(n_clus, n_src, embeddings.shape[0]):
            return one_kernel(n_clus, n_src, embeddings, cluster)
        return on_device(embeddings, cluster)

    placed = (P(("clus", "src"), None), P(("clus", "src")))
    return jax.shard_map(
        body,
        mesh=mesh,
        in_specs=placed,
        out_specs=(P("clus", None), P(("clus", "src"))),
        check_vma=False,
    )
```

```python
import functools

import jax
import jax.numpy as jnp
from jax import lax
from jax.experimental import pallas as pl
from jax.experimental.pallas import tpu as pltpu
from jax.sharding import PartitionSpec as P

CLUS_DEV = 8
MESH = pl.DeviceIdType.MESH
EPS = 1e-06
LOADS = 4


def partner(index, distance, count):
    total = 0
    bit = 1
    while bit < count:
        value = (index // bit) % 2
        total = total + bit * ((1 - value) if (distance // bit) % 2 else value)
        bit *= 2
    return total


def exact_parts(values):
    high = values.astype(jnp.bfloat16)
    rest = values - high.astype(jnp.float32)
    middle = rest.astype(jnp.bfloat16)
    low = (rest - middle.astype(jnp.float32)).astype(jnp.bfloat16)
    return high, middle, low


def dot_t(left, right):
    return lax.dot_general(left, right, (((1,), (1,)), ((), ())), preferred_element_type=jnp.float32)


def xor(left, right, count):
    total = 0
    bit = 1
    while bit < count:
        a, b = (left // bit) % 2, (right // bit) % 2
        total = total + bit * (a + b - 2 * a * b)
        bit *= 2
    return total


def hub_kernel(
    n_clus,
    n_src,
    cap,
    cluster_hbm,
    emb_hbm,
    cent_ref,
    near_ref,
    cluster_ref,
    emb_ref,
    packed,
    gathered,
    label_out,
    labels,
    group_labels,
    best,
    maxima,
    partial,
    partial_in,
    owned,
    owned_in,
    cents,
    row_send,
    row_recv,
    label_send,
    label_recv,
    max_send,
    max_recv,
    partial_sem,
    owned_sem,
    cent_sem,
    load_sem,
):
    rows, depth = emb_ref.shape
    slots = n_clus * cap
    per = CLUS_DEV // n_src
    me = lax.axis_index("clus")
    src = lax.axis_index("src")
    plane, side, level = me // 2, me % 2, src // 2
    is_hub = (src % 2 == 0) & (plane >= 1) & (plane <= 2)
    my_owner = (plane - 1) * 4 + level * 2 + side
    at_clus = [(partner(me, d, n_clus), src) for d in range(n_clus)]
    at_src = [(me, partner(src, e, n_src)) for e in range(n_src)]
    everyone = [
        (d, e, (partner(me, d, n_clus), partner(src, e, n_src)))
        for d in range(n_clus)
        for e in range(n_src)
    ]

    def copy(source, target, send, recv, device):
        return pltpu.make_async_remote_copy(
            src_ref=source,
            dst_ref=target,
            send_sem=send,
            recv_sem=recv,
            device_id=device,
            device_id_type=MESH,
        )

    def paired(source, target, sems, slot, device):
        return copy(source, target, sems.at[0, slot], sems.at[1, slot], device)

    band = rows // LOADS
    load_rows = [
        pltpu.make_async_copy(
            emb_hbm.at[pl.ds(i * band, band)], emb_ref.at[pl.ds(i * band, band)], load_sem.at[1 + i]
        )
        for i in range(LOADS)
    ]
    load_cluster = pltpu.make_async_copy(cluster_hbm, cluster_ref, load_sem.at[0])
    load_cluster.start()
    for load in load_rows:
        load.start()
    barrier = pltpu.get_barrier_semaphore()
    for _, _, device in everyone[1:]:
        pl.semaphore_signal(barrier, inc=1, device_id=device, device_id_type=MESH)

    load_cluster.wait()
    cluster = cluster_ref[...]
    within = cluster % CLUS_DEV
    owner = cluster // CLUS_DEV
    hits = lax.broadcasted_iota(jnp.int32, (n_clus, rows), 0) == owner
    earlier = lax.broadcasted_iota(jnp.int32, (rows, rows), 0) < lax.broadcasted_iota(
        jnp.int32, (rows, rows), 1
    )
    before = jnp.dot(
        jnp.where(hits, 1.0, 0.0).astype(jnp.bfloat16),
        jnp.where(earlier, 1.0, 0.0).astype(jnp.bfloat16),
        preferred_element_type=jnp.float32,
    )
    place = jnp.sum(jnp.where(hits, before, 0.0), axis=0, keepdims=True).astype(jnp.int32)
    slot_rows = lax.broadcasted_iota(jnp.int32, (slots, rows), 0)
    pick = jnp.where(slot_rows == owner * cap + place, 1.0, 0.0).astype(jnp.bfloat16)
    block = jnp.bitwise_xor(owner % 2, side) * n_src + jnp.bitwise_xor(
        (owner // 2) % 2 * 2, src
    )
    spread = jnp.where(slot_rows == block * cap + place, 1.0, 0.0).astype(jnp.bfloat16)
    marked = jnp.where(hits, (within + 1).astype(jnp.float32), 0.0).astype(jnp.bfloat16)
    label_rows = dot_t(marked, spread)
    for o in range(n_clus):
        label_out[o] = label_rows[o : o + 1]

    units = []
    for i, load in enumerate(load_rows):
        load.wait()
        part = emb_ref[i * band : (i + 1) * band]
        norm = lax.rsqrt(jnp.sum(part * part, axis=1, keepdims=True) + EPS)
        units.append((part * norm).astype(jnp.bfloat16))
    unit = jnp.concatenate(units, axis=0)
    packed[...] = (
        jnp.dot(pick, unit, preferred_element_type=jnp.float32)
        .astype(jnp.bfloat16)
        .reshape(n_clus, cap, depth)
    )

    near_plane = plane // 2
    row_copy, label_copy, homes = [], [], []
    for i in range(n_clus):
        z = near_plane if i % 2 else 1 - near_plane
        x = partner(side, (i // 2) % 2, 2)
        y = partner(level, i // 4, 2)
        o = z * 4 + y * 2 + x
        device = ((1 + z) * 2 + x, 2 * y)
        d, e = xor(me, device[0], n_clus), xor(src, device[1], n_src)
        homes.append(o)
        row_copy.append(
            copy(packed.at[o], gathered.at[d, e], row_send.at[i], row_recv.at[d, e], device)
        )
        label_copy.append(
            copy(label_out.at[o], labels.at[d, e], label_send.at[i], label_recv.at[d, e], device)
        )
    partial_copy = [
        paired(partial.at[1], partial_in.at[0], partial_sem, 0, at_src[1]),
        paired(partial.at[3], partial_in.at[1], partial_sem, 1, at_src[1]),
        paired(partial.at[2], partial_in.at[2], partial_sem, 2, at_src[2]),
    ]
    owned_copy = {
        d: paired(owned.at[d], owned_in.at[d], owned_sem, d, at_clus[d]) for d in range(1, n_clus)
    }
    cent_copy = {
        e: paired(cents.at[0], cents.at[e], cent_sem, e, at_src[e]) for e in range(1, n_src)
    }

    pl.semaphore_wait(barrier, len(everyone) - 1)
    def send(copies, places):
        for i in places:
            if i == 1:
                @pl.when(jnp.logical_not(is_hub))
                def _():
                    copies[1].start()
            else:
                copies[i].start()

    send(label_copy, range(n_clus))
    send(row_copy, range(4))

    @pl.when(is_hub)
    def _():
        gathered[0, 0] = packed[homes[1]]
        labels[0, 0] = label_out[homes[1]]

    order = (
        jnp.bitwise_xor(within // per, src) * (n_clus * per)
        + jnp.bitwise_xor(owner, me) * per
        + within % per
    )
    count = n_src * n_clus * per
    members = jnp.where(
        lax.broadcasted_iota(jnp.int32, (count, rows), 0) == order, 2.0, 0.0
    ).astype(jnp.bfloat16)
    sums = jnp.zeros((count, depth), jnp.float32)
    for part in exact_parts(emb_ref[...] * 0.5):
        sums = sums + jnp.dot(members, part, preferred_element_type=jnp.float32)
    partial[...] = sums.reshape(n_src, n_clus * per, depth)
    partial_copy[0].start()
    partial_copy[1].start()
    send(row_copy, range(4, 6))
    partial_copy[0].wait_recv()
    partial_copy[1].wait_recv()
    partial[2] = partial[2] + partial_in[1]
    partial_copy[2].start()
    send(row_copy, range(6, n_clus))
    partial_copy[2].wait_recv()
    total = partial[0] + partial_in[0] + partial_in[2]
    for d in range(n_clus):
        owned[d] = total[d * per : (d + 1) * per]
    for d in range(1, n_clus):
        owned_copy[d].start()

    def arrived(copy_source, target, sems, d, e):
        copy(copy_source, target.at[d, e], sems.at[d, e], sems.at[d, e], at_src[1]).wait_recv()

    def meet(group, earlier_groups):
        width = 2 * n_src * cap
        mine = jnp.zeros((1, width), jnp.float32)
        for d in (2 * group, 2 * group + 1):
            for e in range(n_src):
                if d or e:
                    arrived(label_out.at[0], labels, label_recv, d, e)
                mine = mine + labels[d, e]
        group_labels[group] = mine
        column = jnp.transpose(jnp.broadcast_to(mine, (128, width)))
        column = jnp.concatenate([column] * (width // 128), axis=1)
        for d in (2 * group, 2 * group + 1):
            for e in range(n_src):
                if d or e:
                    arrived(packed.at[0], gathered, row_recv, d, e)
        left = gathered[2 * group : 2 * group + 2].reshape(width, depth)

        def scores(other):
            right = gathered[2 * other : 2 * other + 2].reshape(width, depth)
            return dot_t(left, right), column == group_labels[other]

        values, allowed = scores(group)
        allowed = allowed & (
            lax.broadcasted_iota(jnp.int32, (width, width), 0)
            != lax.broadcasted_iota(jnp.int32, (width, width), 1)
        )
        top = jnp.max(jnp.where(allowed, values, -1.0), axis=0, keepdims=True)
        across = None
        for other in earlier_groups:
            values, allowed = scores(other)
            values = jnp.where(allowed, values, -1.0)
            best[other] = jnp.maximum(best[other], jnp.max(values, axis=0, keepdims=True))
            for j in range(width // 128):
                piece = values[:, j * 128 : (j + 1) * 128]
                across = piece if across is None else jnp.maximum(across, piece)
        if across is not None:
            top = jnp.maximum(top, jnp.max(jnp.transpose(across), axis=0, keepdims=True))
        best[group] = top

    @pl.when(is_hub)
    def _():
        meet(0, [])
        meet(1, [0])

    def returned(d, e, device):
        return copy(
            best.at[d // 2],
            maxima.at[my_owner],
            max_send.at[d, e],
            max_recv.at[my_owner],
            device,
        )

    @pl.when(is_hub)
    def _():
        meet(3, [0, 1])
        meet(2, [0, 1, 3])
        for d, e, device in everyone[:0:-1]:
            returned(d, e, device).start()
        maxima[my_owner] = best[0]

    total = owned[0]
    for d in range(1, n_clus):
        owned_copy[d].wait_recv()
        total = total + owned_in[d]
    cents[0] = total * lax.rsqrt(jnp.sum(total * total, axis=1, keepdims=True) + EPS)
    for e in range(1, n_src):
        cent_copy[e].start()

    for copies in (label_copy, row_copy):
        for i in range(n_clus):
            if i == 1:
                @pl.when(jnp.logical_not(is_hub))
                def _():
                    copies[1].wait_send()
            else:
                copies[i].wait_send()
    for started in partial_copy + list(owned_copy.values()) + list(cent_copy.values()):
        started.wait_send()
    for e in range(1, n_src):
        cent_copy[e].wait_recv()
    for shard in range(n_src):
        cent_ref[shard * per : (shard + 1) * per, :] = cents[partner(src, shard, n_src)]

    for o in range(n_clus):
        @pl.when(jnp.logical_not(is_hub & (my_owner == o)))
        def _():
            copy(best.at[0], maxima.at[o], max_recv.at[o], max_recv.at[o], at_src[1]).wait_recv()
    near = jnp.zeros((n_clus, rows), jnp.float32)
    for part in exact_parts(jnp.concatenate([maxima[o] for o in range(n_clus)], axis=0)):
        near = near + jnp.dot(part, spread, preferred_element_type=jnp.float32)
    near_ref[...] = jnp.sum(jnp.where(hits, near, 0.0), axis=0, keepdims=True)

    @pl.when(is_hub)
    def _():
        for d, e, device in everyone[1:]:
            returned(d, e, device).wait_send()


def one_kernel(n_clus, n_src, embeddings, cluster):
    rows, depth = embeddings.shape
    cap = 2 * rows // n_clus
    slots = n_clus * cap
    per = CLUS_DEV // n_src
    f32, bf16 = jnp.float32, jnp.bfloat16
    vmem = pl.BlockSpec(memory_space=pltpu.VMEM)
    hbm = pl.BlockSpec(memory_space=pltpu.HBM)
    dma = pltpu.SemaphoreType.DMA
    centroids, nearest = pl.pallas_call(
        functools.partial(hub_kernel, n_clus, n_src, cap),
        out_shape=(
            jax.ShapeDtypeStruct((CLUS_DEV, depth), f32),
            jax.ShapeDtypeStruct((1, rows), f32),
        ),
        in_specs=[hbm, hbm],
        out_specs=(vmem, vmem),
        scratch_shapes=[
            pltpu.VMEM((1, rows), jnp.int32),
            pltpu.VMEM((rows, depth), f32),
            pltpu.VMEM((n_clus, cap, depth), bf16),
            pltpu.VMEM((n_clus, n_src, cap, depth), bf16),
            pltpu.VMEM((n_clus, 1, slots), f32),
            pltpu.VMEM((n_clus, n_src, 1, slots), f32),
            pltpu.VMEM((n_clus // 2, 1, slots), f32),
            pltpu.VMEM((n_clus // 2, 1, slots), f32),
            pltpu.VMEM((n_clus, 1, slots), f32),
            pltpu.VMEM((n_src, n_clus * per, depth), f32),
            pltpu.VMEM((n_src, n_clus * per, depth), f32),
            pltpu.VMEM((n_clus, per, depth), f32),
            pltpu.VMEM((n_clus, per, depth), f32),
            pltpu.VMEM((n_src, per, depth), f32),
            dma((n_clus,)),
            dma((n_clus, n_src)),
            dma((n_clus,)),
            dma((n_clus, n_src)),
            dma((n_clus, n_src)),
            dma((n_clus,)),
            dma((2, n_src)),
            dma((2, n_clus)),
            dma((2, n_src)),
            dma((1 + LOADS,)),
        ],
        compiler_params=pltpu.CompilerParams(
            collective_id=0, has_side_effects=True, vmem_limit_bytes=32 * 1024 * 1024
        ),
        cost_estimate=pl.CostEstimate(
            flops=2 * slots * slots * n_src * depth, bytes_accessed=rows * depth * 4, transcendentals=0
        ),
    )(
        pltpu.with_memory_space_constraint(cluster.reshape(1, rows), pltpu.HBM),
        pltpu.with_memory_space_constraint(embeddings, pltpu.HBM),
    )
    return centroids, nearest.reshape(rows)


def block_maxima(current, own_unit, own_labels, own_global, other_unit, other_labels, other_global):
    scores = lax.dot_general(
        own_unit, other_unit, (((1,), (1,)), ((), ())), preferred_element_type=jnp.float32
    )
    allowed = (
        (own_labels[:, None] == other_labels[None, :])
        & (own_global[:, None] != other_global[None, :])
        & (own_labels[:, None] >= 0)
    )
    return jnp.maximum(current, jnp.max(jnp.where(allowed, scores, jnp.float32(-1.0)), axis=1))


def unit_rows(values):
    return (values * lax.rsqrt(jnp.sum(values * values, axis=1, keepdims=True) + 1e-06)).astype(
        jnp.bfloat16
    )


def normalized(owned):
    return owned * lax.rsqrt(jnp.sum(owned * owned, axis=1, keepdims=True) + 1e-06)


def on_device(embeddings, cluster):
    row_count = embeddings.shape[0]
    feature_dim = embeddings.shape[1]
    clus_count = lax.axis_size("clus")
    source_count = lax.axis_size("src")
    capacity = max(2, 2 * row_count // clus_count)
    slot_total = clus_count * capacity
    owner = cluster // CLUS_DEV
    member_hits = (owner[:, None] == jnp.arange(clus_count, dtype=jnp.int32)[None, :]).astype(
        jnp.int32
    )
    running = jnp.cumsum(member_hits, axis=0)
    position = jnp.sum(member_hits * running, axis=1) - 1
    slot_index = owner * capacity + position
    device_number = lax.axis_index("clus") * source_count + lax.axis_index("src")
    global_row = device_number * row_count + jnp.arange(row_count, dtype=jnp.int32)
    send_labels = jnp.full((slot_total,), -1, jnp.int32).at[slot_index].set(cluster)
    send_global = jnp.full((slot_total,), -1, jnp.int32).at[slot_index].set(global_row)
    count = lax.axis_size("clus") * CLUS_DEV
    inside = (cluster >= 0) & (cluster < count)
    segment = jnp.where(inside, cluster, count)
    owned = lax.psum_scatter(
        jax.ops.segment_sum(embeddings, segment, num_segments=count + 1)[:count],
        "clus",
        scatter_dimension=0,
        tiled=True,
    )
    owned = lax.psum(owned, "src")
    centroids = normalized(owned)
    unit = unit_rows(embeddings)
    send_unit = jnp.zeros((slot_total, feature_dim), jnp.bfloat16).at[slot_index].set(unit)
    received, recv_labels, recv_global = (
        lax.all_to_all(send_unit, "clus", split_axis=0, concat_axis=0, tiled=True),
        lax.all_to_all(send_labels, "clus", split_axis=0, concat_axis=0, tiled=True),
        lax.all_to_all(send_global, "clus", split_axis=0, concat_axis=0, tiled=True),
    )
    initial = jnp.full((slot_total,), -1.0, jnp.float32)
    piece_unit = lax.all_gather(received, "src", axis=0, tiled=True)
    piece_labels = lax.all_gather(recv_labels, "src", axis=0, tiled=True)
    piece_global = lax.all_gather(recv_global, "src", axis=0, tiled=True)
    length = piece_unit.shape[0]
    stacked = (
        piece_unit.reshape(length // slot_total, slot_total, feature_dim),
        piece_labels.reshape(length // slot_total, slot_total),
        piece_global.reshape(length // slot_total, slot_total),
    )

    def stepper(carried, sliced):
        return (
            block_maxima(
                carried, received, recv_labels, recv_global, sliced[0], sliced[1], sliced[2]
            ),
            None,
        )

    result, unused = lax.scan(stepper, initial, stacked)
    returned = lax.all_to_all(result, "clus", split_axis=0, concat_axis=0, tiled=True)
    nearest = returned[slot_index]
    return (centroids, nearest)


def fits_one_kernel(n_clus, n_src, rows):
    return n_clus == 8 and n_src == 4 and rows == 128


def solution(mesh):
    n_clus, n_src = mesh.shape["clus"], mesh.shape["src"]

    def body(embeddings, cluster):
        if fits_one_kernel(n_clus, n_src, embeddings.shape[0]):
            return one_kernel(n_clus, n_src, embeddings, cluster)
        return on_device(embeddings, cluster)

    placed = (P(("clus", "src"), None), P(("clus", "src")))
    return jax.shard_map(
        body,
        mesh=mesh,
        in_specs=placed,
        out_specs=(P("clus", None), P(("clus", "src"))),
        check_vma=False,
    )
```

```python
import functools

import jax
import jax.numpy as jnp
from jax import lax
from jax.experimental import pallas as pl
from jax.experimental.pallas import tpu as pltpu
from jax.sharding import PartitionSpec as P

CLUS_DEV = 8
MESH = pl.DeviceIdType.MESH
EPS = 1e-06
LOADS = 4


def partner(index, distance, count):
    total = 0
    bit = 1
    while bit < count:
        value = (index // bit) % 2
        total = total + bit * ((1 - value) if (distance // bit) % 2 else value)
        bit *= 2
    return total


def exact_parts(values):
    high = values.astype(jnp.bfloat16)
    rest = values - high.astype(jnp.float32)
    middle = rest.astype(jnp.bfloat16)
    low = (rest - middle.astype(jnp.float32)).astype(jnp.bfloat16)
    return high, middle, low


def dot_t(left, right):
    return lax.dot_general(left, right, (((1,), (1,)), ((), ())), preferred_element_type=jnp.float32)


def xor(left, right, count):
    total = 0
    bit = 1
    while bit < count:
        a, b = (left // bit) % 2, (right // bit) % 2
        total = total + bit * (a + b - 2 * a * b)
        bit *= 2
    return total


def hub_kernel(
    n_clus,
    n_src,
    cap,
    cluster_hbm,
    emb_hbm,
    cent_ref,
    near_ref,
    cluster_ref,
    emb_ref,
    packed,
    gathered,
    label_out,
    labels,
    group_labels,
    best,
    maxima,
    partial,
    partial_in,
    owned,
    owned_in,
    cents,
    row_send,
    row_recv,
    label_send,
    label_recv,
    max_send,
    max_recv,
    partial_sem,
    owned_sem,
    cent_sem,
    load_sem,
):
    rows, depth = emb_ref.shape
    slots = n_clus * cap
    per = CLUS_DEV // n_src
    me = lax.axis_index("clus")
    src = lax.axis_index("src")
    plane, side, level = me // 2, me % 2, src // 2
    is_hub = (src % 2 == 0) & (plane >= 1) & (plane <= 2)
    my_owner = (plane - 1) * 4 + level * 2 + side
    at_clus = [(partner(me, d, n_clus), src) for d in range(n_clus)]
    at_src = [(me, partner(src, e, n_src)) for e in range(n_src)]
    everyone = [
        (d, e, (partner(me, d, n_clus), partner(src, e, n_src)))
        for d in range(n_clus)
        for e in range(n_src)
    ]

    def copy(source, target, send, recv, device):
        return pltpu.make_async_remote_copy(
            src_ref=source,
            dst_ref=target,
            send_sem=send,
            recv_sem=recv,
            device_id=device,
            device_id_type=MESH,
        )

    def paired(source, target, sems, slot, device):
        return copy(source, target, sems.at[0, slot], sems.at[1, slot], device)

    band = rows // LOADS
    load_rows = [
        pltpu.make_async_copy(
            emb_hbm.at[pl.ds(i * band, band)], emb_ref.at[pl.ds(i * band, band)], load_sem.at[1 + i]
        )
        for i in range(LOADS)
    ]
    load_cluster = pltpu.make_async_copy(cluster_hbm, cluster_ref, load_sem.at[0])
    load_cluster.start()
    for load in load_rows:
        load.start()
    barrier = pltpu.get_barrier_semaphore()
    for _, _, device in everyone[1:]:
        pl.semaphore_signal(barrier, inc=1, device_id=device, device_id_type=MESH)

    load_cluster.wait()
    cluster = cluster_ref[...]
    within = cluster % CLUS_DEV
    owner = cluster // CLUS_DEV
    hits = lax.broadcasted_iota(jnp.int32, (n_clus, rows), 0) == owner
    earlier = lax.broadcasted_iota(jnp.int32, (rows, rows), 0) < lax.broadcasted_iota(
        jnp.int32, (rows, rows), 1
    )
    before = jnp.dot(
        jnp.where(hits, 1.0, 0.0).astype(jnp.bfloat16),
        jnp.where(earlier, 1.0, 0.0).astype(jnp.bfloat16),
        preferred_element_type=jnp.float32,
    )
    place = jnp.sum(jnp.where(hits, before, 0.0), axis=0, keepdims=True).astype(jnp.int32)
    slot_rows = lax.broadcasted_iota(jnp.int32, (slots, rows), 0)
    pick = jnp.where(slot_rows == owner * cap + place, 1.0, 0.0).astype(jnp.bfloat16)
    block = jnp.bitwise_xor(owner % 2, side) * n_src + jnp.bitwise_xor(
        (owner // 2) % 2 * 2, src
    )
    spread = jnp.where(slot_rows == block * cap + place, 1.0, 0.0).astype(jnp.bfloat16)
    marked = jnp.where(hits, (within + 1).astype(jnp.float32), 0.0).astype(jnp.bfloat16)
    label_rows = dot_t(marked, spread)
    for o in range(n_clus):
        label_out[o] = label_rows[o : o + 1]

    units = []
    for i, load in enumerate(load_rows):
        load.wait()
        part = emb_ref[i * band : (i + 1) * band]
        norm = lax.rsqrt(jnp.sum(part * part, axis=1, keepdims=True) + EPS)
        units.append((part * norm).astype(jnp.bfloat16))
    unit = jnp.concatenate(units, axis=0)
    packed[...] = (
        jnp.dot(pick, unit, preferred_element_type=jnp.float32)
        .astype(jnp.bfloat16)
        .reshape(n_clus, cap, depth)
    )

    near_plane = plane // 2
    row_copy, label_copy, homes = [], [], []
    for i in range(n_clus):
        z = near_plane if i % 2 else 1 - near_plane
        x = partner(side, (i // 2) % 2, 2)
        y = partner(level, i // 4, 2)
        o = z * 4 + y * 2 + x
        device = ((1 + z) * 2 + x, 2 * y)
        d, e = xor(me, device[0], n_clus), xor(src, device[1], n_src)
        homes.append(o)
        row_copy.append(
            copy(packed.at[o], gathered.at[d, e], row_send.at[i], row_recv.at[d, e], device)
        )
        label_copy.append(
            copy(label_out.at[o], labels.at[d, e], label_send.at[i], label_recv.at[d, e], device)
        )
    partial_copy = [
        paired(partial.at[1], partial_in.at[0], partial_sem, 0, at_src[1]),
        paired(partial.at[3], partial_in.at[1], partial_sem, 1, at_src[1]),
        paired(partial.at[2], partial_in.at[2], partial_sem, 2, at_src[2]),
    ]
    owned_copy = {
        d: paired(owned.at[d], owned_in.at[d], owned_sem, d, at_clus[d]) for d in range(1, n_clus)
    }
    cent_copy = {
        e: paired(cents.at[0], cents.at[e], cent_sem, e, at_src[e]) for e in range(1, n_src)
    }

    pl.semaphore_wait(barrier, len(everyone) - 1)
    for copies in (label_copy, row_copy):
        for i in range(n_clus):
            if i == 1:
                @pl.when(jnp.logical_not(is_hub))
                def _():
                    copies[1].start()
            else:
                copies[i].start()

    @pl.when(is_hub)
    def _():
        gathered[0, 0] = packed[homes[1]]
        labels[0, 0] = label_out[homes[1]]

    order = (
        jnp.bitwise_xor(within // per, src) * (n_clus * per)
        + jnp.bitwise_xor(owner, me) * per
        + within % per
    )
    count = n_src * n_clus * per
    members = jnp.where(
        lax.broadcasted_iota(jnp.int32, (count, rows), 0) == order, 2.0, 0.0
    ).astype(jnp.bfloat16)
    sums = jnp.zeros((count, depth), jnp.float32)
    for part in exact_parts(emb_ref[...] * 0.5):
        sums = sums + jnp.dot(members, part, preferred_element_type=jnp.float32)
    partial[...] = sums.reshape(n_src, n_clus * per, depth)
    partial_copy[0].start()
    partial_copy[1].start()
    partial_copy[0].wait_recv()
    partial_copy[1].wait_recv()
    partial[2] = partial[2] + partial_in[1]
    partial_copy[2].start()
    partial_copy[2].wait_recv()
    total = partial[0] + partial_in[0] + partial_in[2]
    for d in range(n_clus):
        owned[d] = total[d * per : (d + 1) * per]
    for d in range(1, n_clus):
        owned_copy[d].start()

    def arrived(copy_source, target, sems, d, e):
        copy(copy_source, target.at[d, e], sems.at[d, e], sems.at[d, e], at_src[1]).wait_recv()

    def meet(group, earlier_groups):
        width = 2 * n_src * cap
        mine = jnp.zeros((1, width), jnp.float32)
        for d in (2 * group, 2 * group + 1):
            for e in range(n_src):
                if d or e:
                    arrived(label_out.at[0], labels, label_recv, d, e)
                mine = mine + labels[d, e]
        group_labels[group] = mine
        column = jnp.transpose(jnp.broadcast_to(mine, (128, width)))
        column = jnp.concatenate([column] * (width // 128), axis=1)
        for d in (2 * group, 2 * group + 1):
            for e in range(n_src):
                if d or e:
                    arrived(packed.at[0], gathered, row_recv, d, e)
        left = gathered[2 * group : 2 * group + 2].reshape(width, depth)

        def scores(other):
            right = gathered[2 * other : 2 * other + 2].reshape(width, depth)
            return dot_t(left, right), column == group_labels[other]

        values, allowed = scores(group)
        allowed = allowed & (
            lax.broadcasted_iota(jnp.int32, (width, width), 0)
            != lax.broadcasted_iota(jnp.int32, (width, width), 1)
        )
        top = jnp.max(jnp.where(allowed, values, -1.0), axis=0, keepdims=True)
        across = None
        for other in earlier_groups:
            values, allowed = scores(other)
            values = jnp.where(allowed, values, -1.0)
            best[other] = jnp.maximum(best[other], jnp.max(values, axis=0, keepdims=True))
            for j in range(width // 128):
                piece = values[:, j * 128 : (j + 1) * 128]
                across = piece if across is None else jnp.maximum(across, piece)
        if across is not None:
            top = jnp.maximum(top, jnp.max(jnp.transpose(across), axis=0, keepdims=True))
        best[group] = top

    @pl.when(is_hub)
    def _():
        meet(0, [])
        meet(1, [0])

    total = owned[0]
    for d in range(1, n_clus):
        owned_copy[d].wait_recv()
        total = total + owned_in[d]
    cents[0] = total * lax.rsqrt(jnp.sum(total * total, axis=1, keepdims=True) + EPS)
    for e in range(1, n_src):
        cent_copy[e].start()

    def returned(d, e, device):
        return copy(
            best.at[d // 2],
            maxima.at[my_owner],
            max_send.at[d, e],
            max_recv.at[my_owner],
            device,
        )

    @pl.when(is_hub)
    def _():
        meet(3, [0, 1])
        meet(2, [0, 1, 3])
        for d, e, device in everyone[:0:-1]:
            returned(d, e, device).start()
        maxima[my_owner] = best[0]

    for copies in (label_copy, row_copy):
        for i in range(n_clus):
            if i == 1:
                @pl.when(jnp.logical_not(is_hub))
                def _():
                    copies[1].wait_send()
            else:
                copies[i].wait_send()
    for started in partial_copy + list(owned_copy.values()) + list(cent_copy.values()):
        started.wait_send()
    for e in range(1, n_src):
        cent_copy[e].wait_recv()
    for shard in range(n_src):
        cent_ref[shard * per : (shard + 1) * per, :] = cents[partner(src, shard, n_src)]

    for o in range(n_clus):
        @pl.when(jnp.logical_not(is_hub & (my_owner == o)))
        def _():
            copy(best.at[0], maxima.at[o], max_recv.at[o], max_recv.at[o], at_src[1]).wait_recv()
    near = jnp.zeros((n_clus, rows), jnp.float32)
    for part in exact_parts(jnp.concatenate([maxima[o] for o in range(n_clus)], axis=0)):
        near = near + jnp.dot(part, spread, preferred_element_type=jnp.float32)
    near_ref[...] = jnp.sum(jnp.where(hits, near, 0.0), axis=0, keepdims=True)

    @pl.when(is_hub)
    def _():
        for d, e, device in everyone[1:]:
            returned(d, e, device).wait_send()


def store_kernel(cent_ref, near_ref, cent_hbm, near_hbm, sem):
    stores = [
        pltpu.make_async_copy(cent_ref, cent_hbm, sem.at[0]),
        pltpu.make_async_copy(near_ref, near_hbm, sem.at[1]),
    ]
    for store in stores:
        store.start()
    for store in stores:
        store.wait()


def one_kernel(n_clus, n_src, embeddings, cluster):
    rows, depth = embeddings.shape
    cap = 2 * rows // n_clus
    slots = n_clus * cap
    per = CLUS_DEV // n_src
    f32, bf16 = jnp.float32, jnp.bfloat16
    vmem = pl.BlockSpec(memory_space=pltpu.VMEM)
    hbm = pl.BlockSpec(memory_space=pltpu.HBM)
    dma = pltpu.SemaphoreType.DMA
    centroids, nearest = pl.pallas_call(
        functools.partial(hub_kernel, n_clus, n_src, cap),
        out_shape=(
            jax.ShapeDtypeStruct((CLUS_DEV, depth), f32),
            jax.ShapeDtypeStruct((1, rows), f32),
        ),
        in_specs=[hbm, hbm],
        out_specs=(vmem, vmem),
        scratch_shapes=[
            pltpu.VMEM((1, rows), jnp.int32),
            pltpu.VMEM((rows, depth), f32),
            pltpu.VMEM((n_clus, cap, depth), bf16),
            pltpu.VMEM((n_clus, n_src, cap, depth), bf16),
            pltpu.VMEM((n_clus, 1, slots), f32),
            pltpu.VMEM((n_clus, n_src, 1, slots), f32),
            pltpu.VMEM((n_clus // 2, 1, slots), f32),
            pltpu.VMEM((n_clus // 2, 1, slots), f32),
            pltpu.VMEM((n_clus, 1, slots), f32),
            pltpu.VMEM((n_src, n_clus * per, depth), f32),
            pltpu.VMEM((n_src, n_clus * per, depth), f32),
            pltpu.VMEM((n_clus, per, depth), f32),
            pltpu.VMEM((n_clus, per, depth), f32),
            pltpu.VMEM((n_src, per, depth), f32),
            dma((n_clus,)),
            dma((n_clus, n_src)),
            dma((n_clus,)),
            dma((n_clus, n_src)),
            dma((n_clus, n_src)),
            dma((n_clus,)),
            dma((2, n_src)),
            dma((2, n_clus)),
            dma((2, n_src)),
            dma((1 + LOADS,)),
        ],
        compiler_params=pltpu.CompilerParams(
            collective_id=0, has_side_effects=True, vmem_limit_bytes=32 * 1024 * 1024
        ),
        cost_estimate=pl.CostEstimate(
            flops=2 * slots * slots * n_src * depth, bytes_accessed=rows * depth * 4, transcendentals=0
        ),
    )(
        pltpu.with_memory_space_constraint(cluster.reshape(1, rows), pltpu.HBM),
        pltpu.with_memory_space_constraint(embeddings, pltpu.HBM),
    )
    centroids, nearest = pl.pallas_call(
        store_kernel,
        out_shape=(
            jax.ShapeDtypeStruct((CLUS_DEV, depth), f32),
            jax.ShapeDtypeStruct((1, rows), f32),
        ),
        in_specs=[vmem, vmem],
        out_specs=(hbm, hbm),
        scratch_shapes=[dma((2,))],
    )(centroids, nearest)
    return centroids, nearest.reshape(rows)


def block_maxima(current, own_unit, own_labels, own_global, other_unit, other_labels, other_global):
    scores = lax.dot_general(
        own_unit, other_unit, (((1,), (1,)), ((), ())), preferred_element_type=jnp.float32
    )
    allowed = (
        (own_labels[:, None] == other_labels[None, :])
        & (own_global[:, None] != other_global[None, :])
        & (own_labels[:, None] >= 0)
    )
    return jnp.maximum(current, jnp.max(jnp.where(allowed, scores, jnp.float32(-1.0)), axis=1))


def unit_rows(values):
    return (values * lax.rsqrt(jnp.sum(values * values, axis=1, keepdims=True) + 1e-06)).astype(
        jnp.bfloat16
    )


def normalized(owned):
    return owned * lax.rsqrt(jnp.sum(owned * owned, axis=1, keepdims=True) + 1e-06)


def on_device(embeddings, cluster):
    row_count = embeddings.shape[0]
    feature_dim = embeddings.shape[1]
    clus_count = lax.axis_size("clus")
    source_count = lax.axis_size("src")
    capacity = max(2, 2 * row_count // clus_count)
    slot_total = clus_count * capacity
    owner = cluster // CLUS_DEV
    member_hits = (owner[:, None] == jnp.arange(clus_count, dtype=jnp.int32)[None, :]).astype(
        jnp.int32
    )
    running = jnp.cumsum(member_hits, axis=0)
    position = jnp.sum(member_hits * running, axis=1) - 1
    slot_index = owner * capacity + position
    device_number = lax.axis_index("clus") * source_count + lax.axis_index("src")
    global_row = device_number * row_count + jnp.arange(row_count, dtype=jnp.int32)
    send_labels = jnp.full((slot_total,), -1, jnp.int32).at[slot_index].set(cluster)
    send_global = jnp.full((slot_total,), -1, jnp.int32).at[slot_index].set(global_row)
    count = lax.axis_size("clus") * CLUS_DEV
    inside = (cluster >= 0) & (cluster < count)
    segment = jnp.where(inside, cluster, count)
    owned = lax.psum_scatter(
        jax.ops.segment_sum(embeddings, segment, num_segments=count + 1)[:count],
        "clus",
        scatter_dimension=0,
        tiled=True,
    )
    owned = lax.psum(owned, "src")
    centroids = normalized(owned)
    unit = unit_rows(embeddings)
    send_unit = jnp.zeros((slot_total, feature_dim), jnp.bfloat16).at[slot_index].set(unit)
    received, recv_labels, recv_global = (
        lax.all_to_all(send_unit, "clus", split_axis=0, concat_axis=0, tiled=True),
        lax.all_to_all(send_labels, "clus", split_axis=0, concat_axis=0, tiled=True),
        lax.all_to_all(send_global, "clus", split_axis=0, concat_axis=0, tiled=True),
    )
    initial = jnp.full((slot_total,), -1.0, jnp.float32)
    piece_unit = lax.all_gather(received, "src", axis=0, tiled=True)
    piece_labels = lax.all_gather(recv_labels, "src", axis=0, tiled=True)
    piece_global = lax.all_gather(recv_global, "src", axis=0, tiled=True)
    length = piece_unit.shape[0]
    stacked = (
        piece_unit.reshape(length // slot_total, slot_total, feature_dim),
        piece_labels.reshape(length // slot_total, slot_total),
        piece_global.reshape(length // slot_total, slot_total),
    )

    def stepper(carried, sliced):
        return (
            block_maxima(
                carried, received, recv_labels, recv_global, sliced[0], sliced[1], sliced[2]
            ),
            None,
        )

    result, unused = lax.scan(stepper, initial, stacked)
    returned = lax.all_to_all(result, "clus", split_axis=0, concat_axis=0, tiled=True)
    nearest = returned[slot_index]
    return (centroids, nearest)


def fits_one_kernel(n_clus, n_src, rows):
    return n_clus == 8 and n_src == 4 and rows == 128


def solution(mesh):
    n_clus, n_src = mesh.shape["clus"], mesh.shape["src"]

    def body(embeddings, cluster):
        if fits_one_kernel(n_clus, n_src, embeddings.shape[0]):
            return one_kernel(n_clus, n_src, embeddings, cluster)
        return on_device(embeddings, cluster)

    placed = (P(("clus", "src"), None), P(("clus", "src")))
    return jax.shard_map(
        body,
        mesh=mesh,
        in_specs=placed,
        out_specs=(P("clus", None), P(("clus", "src"))),
        check_vma=False,
    )
```
